128 devices in a mesh: seg: 16 (over y, x), head: 8 (over z, core).
Axes of the slice: x: 4, y: 4, z: 4, core: 2. Of those that a mesh axis runs over, the one named last changes fastest.
Arguments:
- queries: bfloat16 [128, 256, 5120], P(('seg', 'head')), may hold values from -6 to 6
- key_states: bfloat16 [128, 256, 1024], P(('seg', 'head')), may hold values from -6 to 6
- values: bfloat16 [128, 256, 1024], P(('seg', 'head')), may hold values from -6 to 6
- grad_out: bfloat16 [128, 256, 5120], P(('seg', 'head')), may hold values from -6 to 6
- owners: int32 [128], replicated, may hold values from 0 to 127, as said below
- parents: int32 [128], replicated, may hold values from -1 to 31, as said below
- depths: int32 [128], replicated, may hold values from 0 to 2, as said below
- lengths: int32 [128], replicated, may hold values from 64 to 256, as said below
Outputs:
- query_grads: bfloat16 [128, 256, 5120], P(('seg', 'head'))
- key_grads: bfloat16 [128, 256, 1024], P(('seg', 'head'))
- value_grads: bfloat16 [128, 256, 1024], P(('seg', 'head'))
The draws below stay inside these ranges and needn't reach their ends.
Inputs may be any that keep to these rules, and one draw needn't show every extreme that they name: A permutation: segment g sits in slot owners[g], on the index owners[g] // 8 of seg; each index of seg holds exactly 2 segments that have children. -1 exactly for the 8 roots, segments 0 to 7; any other segment's parent has a smaller number; segments 8 to 31 have roots as parents; every segment below 32 has a child and none from 32 on. `depths`: the number of ancestors: 0 for roots, else one more than the parent's. The first lengths[g] positions of a segment's slot are tokens, the rest padding.
All inputs are finite; a program needn't handle non-finite values.
Results may differ from the reference program's by a relative error of at most 0.014.
Values may be sent and summed in bfloat16 or wider, within the bound.
A program may use at most 128 MiB of HBM per device.

```python
import jax
import jax.numpy as jnp
from jax import lax

QH = 40
KVH = 8
DH = 128
SEG_DEV = 8
SLOT = 256
PUB = 2
NSEG = 128
NINT = 32
NROOT = 8
N_SEG = 16


def tree_draw(key):
    key = jax.random.fold_in(key, 202)
    device_count = NSEG // SEG_DEV
    subkeys = jax.random.split(key, 6)
    segment_ids = jnp.arange(NSEG, dtype=jnp.int32)
    first_level = NINT - NROOT
    root_order = jax.random.permutation(subkeys[0], NROOT).astype(jnp.int32)
    middle_order = jax.random.permutation(subkeys[1], first_level).astype(jnp.int32)
    random_root = jax.random.randint(subkeys[2], (NSEG,), 0, NROOT)
    random_inner = jax.random.randint(subkeys[3], (NSEG,), 0, NINT)
    middle = segment_ids - NROOT
    middle_parent = jnp.where(middle < NROOT, root_order[jnp.clip(middle, 0, NROOT - 1)], random_root)
    leaf_index = segment_ids - NINT
    leaf_parent = jnp.where(leaf_index < first_level, NROOT + middle_order[jnp.clip(leaf_index, 0, first_level - 1)], random_inner)
    parents = jnp.where(segment_ids < NROOT, -1, jnp.where(segment_ids < NINT, middle_parent, leaf_parent)).astype(jnp.int32)
    depths = jnp.where(segment_ids < NROOT, 0, jnp.where(segment_ids < NINT, 1, jnp.where(parents < NROOT, 1, 2))).astype(jnp.int32)
    round_of = jnp.where(segment_ids < NINT, segment_ids // device_count, PUB + (segment_ids - NINT) // device_count)
    position_in = jnp.where(segment_ids < NINT, segment_ids % device_count, (segment_ids - NINT) % device_count)
    device_orders = jax.vmap(lambda sub: jax.random.permutation(sub, device_count))(jax.random.split(subkeys[4], SEG_DEV)).astype(jnp.int32)
    local_orders = jax.vmap(lambda sub: jax.random.permutation(sub, SEG_DEV))(jax.random.split(subkeys[5], device_count)).astype(jnp.int32)
    device_pick = device_orders[round_of, position_in]
    local_slot = local_orders[device_pick, round_of]
    owners = (device_pick * SEG_DEV + local_slot).astype(jnp.int32)
    return (owners, parents, depths)


def draw_owners(key, part):
    return tree_draw(key)[0]


def draw_parents(key, part):
    return tree_draw(key)[1]


def draw_depths(key, part):
    return tree_draw(key)[2]


def draw_lengths(key, part):
    key = jax.random.fold_in(key, 3)
    subkeys = jax.random.split(key, 3)
    drawn = jax.random.randint(subkeys[0], (NSEG,), SLOT // 4, SLOT + 1)
    full_at = jax.random.randint(subkeys[1], (), 0, NSEG)
    short_at = (full_at + 1 + jax.random.randint(subkeys[2], (), 0, NSEG - 1)) % NSEG
    drawn = drawn.at[full_at].set(SLOT).at[short_at].set(SLOT // 4)
    return drawn.astype(jnp.int32)


def draw_queries(key, part):
    key = jax.random.fold_in(key, 5)
    drawn = jnp.clip(jax.random.normal(key, (NSEG, SLOT, QH * DH), jnp.float32), -6.0, 6.0)
    return drawn.astype(jnp.bfloat16)


def draw_key_states(key, part):
    key = jax.random.fold_in(key, 7)
    drawn = jnp.clip(jax.random.normal(key, (NSEG, SLOT, KVH * DH), jnp.float32), -6.0, 6.0)
    return drawn.astype(jnp.bfloat16)


def steps_of(own_key, shape, shards, least, top_value):
    level = 1.0
    for position, parts in shards:
        heights = jax.random.uniform(jax.random.fold_in(jax.random.fold_in(own_key, 6), position), (parts,), jnp.float32, least / len(shards), top_value / len(shards))
        level = level * jnp.repeat(jnp.exp(heights), shape[position] // parts).reshape((-1,) + (1,) * (len(shape) - 1 - position))
    return level


def gaussian(own_key, dims, scale, most, cuts=(), held_as=jnp.bfloat16):
    array = jax.random.normal(own_key, dims, jnp.float32) * scale
    if len(cuts) > 0:
        array = steps_of(own_key, dims, cuts, -0.22, 0.18) * array
    return jnp.clip(array, min=-most, max=most).astype(held_as)


def setup_inputs(seed: int = 0) -> dict:
    splits = jax.random.split(jax.random.key(seed), 9)
    return {
        "queries": draw_queries(jax.random.fold_in(splits[8], 71), 0),
        "key_states": draw_key_states(jax.random.fold_in(splits[8], 71), 0),
        "values": gaussian(splits[2], (NSEG, SLOT, KVH * DH), 1.0, 6.0, ((0, 128),)),
        "grad_out": gaussian(splits[3], (NSEG, SLOT, QH * DH), 1.0, 6.0, ((0, 128),)),
        "owners": draw_owners(jax.random.fold_in(splits[8], 71), 0),
        "parents": draw_parents(jax.random.fold_in(splits[8], 71), 0),
        "depths": draw_depths(jax.random.fold_in(splits[8], 71), 0),
        "lengths": draw_lengths(jax.random.fold_in(splits[8], 71), 0),
    }


def lookup(source_table, wanted):
    places = jnp.arange(source_table.shape[0], dtype=jnp.int32)
    picked = jnp.where(wanted[:, None] == places[None, :], source_table[None, :], 0)
    return jnp.sum(picked, axis=1).astype(jnp.int32)


def tree_tables(owners, parents, depths, lengths, per_device, published):
    count_all = owners.shape[0]
    slot_ids = jnp.arange(count_all, dtype=jnp.int32)
    segment_at = jnp.sum(jnp.where(owners[None, :] == slot_ids[:, None], slot_ids[None, :], 0), axis=1).astype(jnp.int32)
    first_up = lookup(parents, segment_at)
    second_up = lookup(parents, jnp.maximum(first_up, 0))
    levels = lookup(depths, segment_at)
    valid_one = (levels >= 1) & (first_up >= 0)
    valid_two = (levels >= 2) & valid_one & (second_up >= 0)
    slot_one = lookup(owners, jnp.maximum(first_up, 0))
    slot_two = lookup(owners, jnp.maximum(second_up, 0))
    own_length = lookup(lengths, segment_at)
    length_one = lookup(lengths, jnp.maximum(first_up, 0))
    length_two = lookup(lengths, jnp.maximum(second_up, 0))
    pointed = jnp.any(((slot_one[:, None] == slot_ids[None, :]) & valid_one[:, None])
                      | ((slot_two[:, None] == slot_ids[None, :]) & valid_two[:, None]), axis=0)
    device_of = slot_ids // per_device
    earlier = (device_of[None, :] == device_of[:, None]) & (slot_ids[None, :] < slot_ids[:, None]) & pointed[None, :]
    ranking = jnp.sum(earlier.astype(jnp.int32), axis=1).astype(jnp.int32)
    shared_index = (device_of * published + ranking).astype(jnp.int32)
    return (own_length, slot_one, slot_two, valid_one, valid_two, length_one, length_two, pointed, ranking, shared_index)


def reference(queries, key_states, values, grad_out, owners, parents, depths, lengths):
    tables = tree_tables(owners, parents, depths, lengths, SEG_DEV, PUB)
    own_length, slot_one, slot_two, valid_one, valid_two, length_one, length_two = tables[:7]
    group_size = QH // KVH
    softmax_scale = DH ** -0.5
    rows = jnp.arange(SLOT, dtype=jnp.int32)
    columns = jnp.arange(3 * SLOT, dtype=jnp.int32)
    column_block = columns // SLOT
    column_inner = columns % SLOT

    def visit(carry, slot):
        key_sums, value_sums, key_far, value_far = carry
        first_slot = slot_one[slot]
        second_slot = slot_two[slot]
        key_cat = jnp.concatenate([key_states[slot], key_states[first_slot], key_states[second_slot]], axis=0)
        key_cat = key_cat.astype(jnp.float32).reshape(3 * SLOT, KVH, DH)
        value_cat = jnp.concatenate([values[slot], values[first_slot], values[second_slot]], axis=0)
        value_cat = value_cat.astype(jnp.float32).reshape(3 * SLOT, KVH, DH)
        query_heads = queries[slot].astype(jnp.float32).reshape(SLOT, KVH, group_size, DH)
        length_here = own_length[slot]
        own_allowed = (column_inner[None, :] <= rows[:, None]) & (column_inner[None, :] < length_here)
        first_allowed = (column_inner[None, :] < length_one[slot]) & valid_one[slot]
        second_allowed = (column_inner[None, :] < length_two[slot]) & valid_two[slot]
        allowed = jnp.where(column_block[None, :] == 0, own_allowed,
                            jnp.where(column_block[None, :] == 1, first_allowed, second_allowed))
        live = rows < length_here
        gated = jnp.where(live[:, None], grad_out[slot], jnp.zeros_like(grad_out[slot]))
        gated = gated.astype(jnp.float32).reshape(SLOT, KVH, group_size, DH)
        scores = jnp.einsum("tkgd,ukd->kgtu", query_heads, key_cat) * softmax_scale
        scores = jnp.where(allowed, scores, -1e30)
        highest = jnp.max(scores, axis=-1, keepdims=True)
        log_total = highest + jnp.log(jnp.sum(jnp.exp(scores - highest), axis=-1, keepdims=True))
        weights = jnp.exp(scores - log_total)
        weights_low = lax.optimization_barrier(weights.astype(jnp.bfloat16)).astype(jnp.float32)
        attended = jnp.einsum("kgtu,ukd->tkgd", weights_low, value_cat)
        deltas = jnp.sum(gated * attended, axis=-1)
        weight_grads = jnp.einsum("tkgd,ukd->kgtu", gated, value_cat)
        score_grads = weights * (weight_grads - jnp.transpose(deltas, (1, 2, 0))[..., None])
        score_low = lax.optimization_barrier(score_grads.astype(jnp.bfloat16)).astype(jnp.float32)
        query_grads = softmax_scale * jnp.einsum("kgtu,ukd->tkgd", score_low, key_cat)
        query_grads = query_grads.astype(jnp.bfloat16).reshape(SLOT, QH * DH)
        key_part = (softmax_scale * jnp.einsum("kgtu,tkgd->ukd", score_low, query_heads)).reshape(3 * SLOT, KVH * DH)
        value_part = jnp.einsum("kgtu,tkgd->ukd", weights_low, gated).reshape(3 * SLOT, KVH * DH)
        key_sums = key_sums.at[slot].add(key_part[:SLOT])
        value_sums = value_sums.at[slot].add(value_part[:SLOT])
        key_far = key_far.at[first_slot].add(key_part[SLOT:2 * SLOT]).at[second_slot].add(key_part[2 * SLOT:])
        value_far = value_far.at[first_slot].add(value_part[SLOT:2 * SLOT]).at[second_slot].add(value_part[2 * SLOT:])
        return (key_sums, value_sums, key_far, value_far), query_grads

    zeros_start = jnp.zeros((NSEG, SLOT, KVH * DH), jnp.float32)

    def device_pass(carry, device):
        key_sums, value_sums = carry
        slots_here = (device * SEG_DEV + jnp.arange(SEG_DEV, dtype=jnp.int32)).astype(jnp.int32)
        (key_sums, value_sums, key_far, value_far), query_grads = lax.scan(
            visit, (key_sums, value_sums, zeros_start, zeros_start), slots_here)
        key_sums = key_sums + lax.optimization_barrier(key_far.astype(jnp.bfloat16)).astype(jnp.float32)
        value_sums = value_sums + lax.optimization_barrier(value_far.astype(jnp.bfloat16)).astype(jnp.float32)
        return (key_sums, value_sums), query_grads

    (key_sums, value_sums), query_grads = lax.scan(device_pass, (zeros_start, zeros_start), jnp.arange(N_SEG, dtype=jnp.int32))
    query_grads = query_grads.reshape(NSEG, SLOT, QH * DH)
    return query_grads, key_sums.astype(jnp.bfloat16), value_sums.astype(jnp.bfloat16)
```

```python
import jax
import jax.numpy as jnp
from jax import lax
from jax.experimental import pallas as pl
from jax.experimental.pallas import tpu as pltpu
from jax.sharding import PartitionSpec as P

DH = 128
PUB = 2
MESH = pl.DeviceIdType.MESH
SIDE = 4
NHEAD = 8
NCOL = 16
BF = jnp.bfloat16
F32 = jnp.float32
NEG = -1e30

T_PUB, T_ANC, T_ORDER, T_CONT, T_LAST, T_RANK, T_OWN = 0, 2, 18, 34, 50, 83, 91
T_SIZE = 96


def table_kernel(owners, parents, depths, lengths, out, inverse, shared):
    col = lax.axis_index("seg")
    mine = lax.axis_index("head")
    count = owners.shape[0]

    def invert(g, carry):
        inverse[owners[g]] = g
        return carry

    lax.fori_loop(0, count, invert, 0)

    def number(slot, rank):
        rank = jnp.where(slot % NHEAD == 0, 0, rank)
        g = inverse[slot]
        inner = g < NCOL * PUB

        @pl.when(inner)
        def _():
            shared[g] = (slot // NHEAD) * PUB + rank

        return rank + inner.astype(jnp.int32)

    lax.fori_loop(0, count, number, 0)
    targets = []
    rank = 0
    for p in range(NHEAD):
        g = inverse[col * NHEAD + p]
        inner = g < NCOL * PUB
        out[T_RANK + p] = jnp.where(inner, rank, 0)

        @pl.when(inner)
        def _():
            out[T_PUB + rank] = p

        rank = rank + inner.astype(jnp.int32)
        up = parents[g]
        depth = depths[g]
        one = (depth >= 1) & (up >= 0)
        up = jnp.maximum(up, 0)
        up2 = parents[up]
        two = (depth >= 2) & one & (up2 >= 0)
        up2 = jnp.maximum(up2, 0)
        first = shared[up]
        second = shared[up2]
        out[T_ANC + 2 * p] = jnp.where(one, first, 0)
        out[T_ANC + 2 * p + 1] = jnp.where(two, second, 0)
        targets.append(jnp.where(one, first, NCOL * PUB))
        targets.append(jnp.where(two, second, NCOL * PUB))

        @pl.when(p == mine)
        def _():
            out[T_OWN] = lengths[g]
            out[T_OWN + 1] = jnp.where(one, lengths[up], 0)
            out[T_OWN + 2] = jnp.where(two, lengths[up2], 0)
            out[T_OWN + 3] = inner.astype(jnp.int32)

    n = len(targets)
    places = [0] * n
    again = [False] * n
    for b in range(n):
        for a in range(b):
            c = targets[a] <= targets[b]
            places[b] = places[b] + c.astype(jnp.int32)
            places[a] = places[a] + 1 - c.astype(jnp.int32)
            again[b] = again[b] | (targets[a] == targets[b])
    for j in range(NCOL * PUB + 1):
        out[T_LAST + j] = n
    for l in range(n):
        out[T_ORDER + places[l]] = l
        out[T_CONT + places[l]] = jnp.int32(0) + again[l]
        out[T_LAST + targets[l]] = places[l]


def tables_of(owners, parents, depths, lengths):
    smem = pl.BlockSpec(memory_space=pltpu.SMEM)
    return pl.pallas_call(
        table_kernel,
        out_shape=jax.ShapeDtypeStruct((T_SIZE,), jnp.int32),
        in_specs=[smem] * 4,
        out_specs=smem,
        scratch_shapes=[pltpu.SMEM((128,), jnp.int32), pltpu.SMEM((32,), jnp.int32)],
    )(owners, parents, depths, lengths)


PEERS = [(0, 1), (1, 0), (3, 0), (1, 1), (3, 1), (2, 0), (2, 1)]


def kernel(tab, q_ref, k_ref, v_ref, g_ref, dq_ref, dk_ref, dv_ref,
           qv, gv, kown, vown, all_k, all_v, sh_k, sh_v, sel_k, sel_v, anc_k, anc_v,
           own_k, own_v, fb_k, fb_v, far_k, far_v, accs_k, accs_v, tt_k, tt_v,
           half_k, half_v, full_k, full_v, fin_k, fin_v, rb_k, rb_v, ret_k, ret_v,
           dqv, bias, live, kc, vc, kt, send_sem, recv_sem, local_sem, out_sem):
    seg = lax.axis_index("seg")
    head = lax.axis_index("head")
    slot = qv.shape[0]
    mid = slot // 2
    y, x = seg // SIDE, seg % SIDE
    z, core = head // 2, head % 2

    def peer(step):
        dz, dc = step
        return ((z + dz) % SIDE) * 2 + (core + dc) % 2

    def along(axis, step):
        if axis == 0:
            return y * SIDE + (x + step) % SIDE
        return ((y + step) % SIDE) * SIDE + x

    def at(axis, da, db):
        if axis == 0:
            return ((y + db) % SIDE) * SIDE + (x + da) % SIDE
        return ((y + da) % SIDE) * SIDE + (x + db) % SIDE

    ids = [0]
    sent = []

    def push(src, dst, to_seg, to_head):
        n = ids[0]
        ids[0] += 1
        copy = pltpu.make_async_remote_copy(
            src_ref=src, dst_ref=dst, send_sem=send_sem.at[n], recv_sem=recv_sem.at[n],
            device_id=(to_seg, to_head), device_id_type=MESH)
        copy.start()
        sent.append(copy)
        return copy

    barrier = pltpu.get_barrier_semaphore()
    for step in PEERS:
        pl.semaphore_signal(barrier, inc=1, device_id=(seg, peer(step)), device_id_type=MESH)
    for axis in (0, 1):
        for step in (1, 3):
            pl.semaphore_signal(barrier, inc=1, device_id=(along(axis, step), head), device_id_type=MESH)
    pl.semaphore_wait(barrier, len(PEERS) + 4)

    def lanes(p):
        return pl.ds(pl.multiple_of(p * DH, DH), DH)

    first = [[], []]
    for kv, (src, dst) in enumerate(((k_ref, all_k), (v_ref, all_v))):
        for step in PEERS:
            p = peer(step)
            first[kv].append(push(src.at[0, :, lanes(p)], dst.at[head], seg, p))
    loads = [
        pltpu.make_async_copy(src.at[0], dst, local_sem.at[n])
        for n, (src, dst) in enumerate(((k_ref, kown), (v_ref, vown), (q_ref, qv), (g_ref, gv)))
    ]
    for load in loads:
        load.start()

    length = tab[T_OWN]
    rows = lax.broadcasted_iota(jnp.int32, (slot, slot), 0)
    cols = lax.broadcasted_iota(jnp.int32, (slot, slot), 1)
    bias[0:slot, :] = jnp.where((rows <= cols) & (rows < length), 0.0, NEG)
    bias[slot:2 * slot, :] = jnp.where(rows < tab[T_OWN + 1], 0.0, NEG)
    bias[2 * slot:3 * slot, :] = jnp.where(rows < tab[T_OWN + 2], 0.0, NEG)
    row = lax.broadcasted_iota(jnp.int32, (slot, DH), 0)
    live[...] = jnp.where(row < length, 1.0, 0.0).astype(BF)

    class Gather:
        def __init__(self, sh, whole, own, arrived):
            self.sh, self.whole, self.own, self.arrived = sh, whole, own, arrived

        def block(self, r, da, db, part=None):
            ref = self.sh.at[at(r, da, db) * PUB + r]
            if part is None:
                return ref
            return ref.at[pl.ds(part * mid, mid)]

        def spread(self, r, axis, da, db):
            ref = self.block(r, da, db)
            return [push(ref, ref, along(axis, 1), head), push(ref, ref, along(axis, 3), head)]

        def relay(self, r, axis, da, db, pair):
            out = []
            for part, copy in enumerate(pair):
                copy.wait_recv()
                step = 3 if part == 0 else 1
                ref = self.block(r, step if axis == r else da, db if axis == r else step, part)
                out.append(push(ref, ref, along(axis, 1 if part == 0 else 3), head))
            return out

        def steps(self):
            for copy in self.arrived:
                copy.wait_recv()
            self.whole[head] = self.own[:, lanes(head)]
            for r in range(PUB):
                self.sh[seg * PUB + r] = self.whole[tab[T_PUB + r]]
            a, b, fa, fb = {}, {}, {}, {}
            for r in range(PUB):
                a[r] = self.spread(r, r, 0, 0)
                b[r, 0] = self.spread(r, 1 - r, 0, 0)
            yield
            for r in range(PUB):
                fa[r] = self.relay(r, r, 0, 0, a[r])
                b[r, 3] = self.spread(r, 1 - r, 3, 0)
                b[r, 1] = self.spread(r, 1 - r, 1, 0)
            yield
            for r in range(PUB):
                fb[r, 0] = self.relay(r, 1 - r, 0, 0, b[r, 0])
            yield
            for r in range(PUB):
                for copy in fa[r]:
                    copy.wait_recv()
                b[r, 2] = self.spread(r, 1 - r, 2, 0)
            for r in range(PUB):
                for da in (3, 1):
                    fb[r, da] = self.relay(r, 1 - r, da, 0, b[r, da])
            yield
            for r in range(PUB):
                fb[r, 2] = self.relay(r, 1 - r, 2, 0, b[r, 2])
            yield
            for pair in fb.values():
                for copy in pair:
                    copy.wait_recv()

    def run(seq):
        for _ in seq:
            return True
        return False

    def select(sh, sel, anc):
        out = {}
        for step in PEERS:
            p = peer(step)
            for a in range(2):
                sel[p * 2 + a] = sh[tab[T_ANC + 2 * p + a]]
            out[step] = push(sel.at[pl.ds(p * 2, 2)], anc.at[pl.ds(head * 2, 2)], seg, p)
        for a in range(2):
            anc[head * 2 + a] = sh[tab[T_ANC + 2 * head + a]]
        return out

    loads[0].wait()
    loads[1].wait()
    gather_k = Gather(sh_k, all_k, kown, first[0]).steps()
    gather_v = Gather(sh_v, all_v, vown, first[1]).steps()
    run(gather_k)
    run(gather_k)
    run(gather_v)
    run(gather_k)
    run(gather_v)
    run(gather_k)
    run(gather_v)
    run(gather_k)
    run(gather_v)
    run(gather_k)
    got_k = select(sh_k, sel_k, anc_k)
    run(gather_v)
    run(gather_v)
    got_v = select(sh_v, sel_v, anc_v)
    loads[2].wait()
    loads[3].wait()

    group = qv.shape[1] // kown.shape[1]
    scale = DH ** -0.5
    exp_scale = scale * 1.4426950408889634
    nt = (((1,), (1,)), ((), ()))
    back = []
    writes = []
    for n, step in enumerate([(0, 0)] + PEERS):
        p = peer(step)
        if n > 0:
            away = ((SIDE - step[0]) % SIDE, step[1])
            got_k[away].wait_recv()
            got_v[away].wait_recv()
        kc[0:slot] = kown[:, lanes(p)]
        vc[0:slot] = vown[:, lanes(p)]
        for a in range(2):
            kc[(a + 1) * slot:(a + 2) * slot] = anc_k[p * 2 + a]
            vc[(a + 1) * slot:(a + 2) * slot] = anc_v[p * 2 + a]
        kt[...] = kc[...].T

        def one(j, carry, p=p):
            dk, dv = carry
            place = lanes(p * group + j)
            q = qv[:, place]
            g = gv[:, place] * live[...]
            s = lax.dot_general(kc[...], q, nt, preferred_element_type=F32) * exp_scale + bias[...]
            top = jnp.max(s, axis=0, keepdims=True)
            e = jnp.exp2(s - top)
            inv = 1.0 / jnp.sum(e, axis=0, keepdims=True)
            wg = lax.dot_general(vc[...], g, nt, preferred_element_type=F32)
            delta = jnp.sum(e * wg, axis=0, keepdims=True) * inv
            ds = (e * (wg - delta)).astype(BF)
            inv_col = jnp.broadcast_to(inv, (DH, slot)).T
            g = (g.astype(F32) * inv_col).astype(BF)
            q = (q.astype(F32) * inv_col).astype(BF)
            dv = dv + jnp.dot(e.astype(BF), g, preferred_element_type=F32)
            dk = dk + jnp.dot(ds, q, preferred_element_type=F32)
            dqt = jnp.dot(kt[...], ds, preferred_element_type=F32) * (inv * scale)
            dqv[:, place] = dqt.T.astype(BF)
            return dk, dv

        zero = jnp.zeros((3 * slot, DH), F32)
        dk, dv = lax.fori_loop(0, group, one, (zero, zero))
        dk = dk * scale
        own_k[p] = dk[0:slot]
        own_v[p] = dv[0:slot]
        wide = pl.ds(pl.multiple_of(p * (group * DH), DH), group * DH)
        write = pltpu.make_async_copy(dqv.at[:, wide], dq_ref.at[0, :, wide], out_sem.at[n])
        write.start()
        writes.append(write)
        fk, fv = (far_k, far_v) if n == 0 else (fb_k, fb_v)
        for a in range(2):
            fk[p * 2 + a] = dk[(a + 1) * slot:(a + 2) * slot].astype(BF)
            fv[p * 2 + a] = dv[(a + 1) * slot:(a + 2) * slot].astype(BF)
        if n > 0:
            back.append(push(fb_k.at[pl.ds(p * 2, 2)], far_k.at[pl.ds(head * 2, 2)], seg, p))
            back.append(push(fb_v.at[pl.ds(p * 2, 2)], far_v.at[pl.ds(head * 2, 2)], seg, p))

    for copy in back:
        copy.wait_recv()
    links = 2 * NHEAD

    def sums(far, accs, tt):
        def add(n, acc):
            acc = far[tab[T_ORDER + n]].astype(F32) + acc * tab[T_CONT + n].astype(F32)
            accs[n] = acc.astype(BF)
            return acc

        lax.fori_loop(0, links, add, jnp.zeros((slot, DH), F32))
        accs[links] = jnp.zeros((slot, DH), BF)

        def spread(j, carry):
            tt[j] = accs[tab[T_LAST + j]]
            return carry

        lax.fori_loop(0, NCOL * PUB, spread, 0)

    def plus(*terms):
        total = terms[0].astype(F32)
        for term in terms[1:]:
            total = total + term.astype(F32)
        return total.astype(BF)

    class Scatter:
        def __init__(self, far, accs, tt, half, full, fin):
            self.far, self.accs, self.tt = far, accs, tt
            self.half, self.full, self.fin = half, full, fin

        def block(self, r, axis, da, db):
            return self.tt.at[at(axis, da, db) * PUB + r]

        def send_far(self, r, axis, other, slot_no):
            ref = self.block(r, axis, 2, other)
            out = []
            for part, step in ((0, 1), (1, 3)):
                out.append(push(ref.at[pl.ds(part * mid, mid)], self.half.at[(r * 5 + slot_no) * 2 + part],
                                along(axis, step), head))
            return out

        def send_near(self, r, axis, other, slot_no, pair):
            out = []
            for part, step in ((0, 1), (1, 3)):
                pair[part].wait_recv()
                ref = self.block(r, axis, step, other)
                span = pl.ds(part * mid, mid)
                ref[span] = plus(ref[span], self.half[(r * 5 + slot_no) * 2 + part])
                out.append(push(ref, self.full.at[(r * 5 + slot_no) * 2 + part], along(axis, step), head))
            return out

        def total(self, r, axis, other, slot_no, pair):
            for copy in pair:
                copy.wait_recv()
            ref = self.block(r, axis, 0, other)
            n = (r * 5 + slot_no) * 2
            return ref, plus(ref[...], self.full[n], self.full[n + 1])

        def steps(self):
            sums(self.far, self.accs, self.tt)
            a, b = {}, {}
            for r in range(PUB):
                for other in (2, 1, 3, 0):
                    a[r, other] = self.send_far(r, 1 - r, other, other)
            yield
            for other in (2, 1, 3, 0):
                for r in range(PUB):
                    b[r, other] = self.send_near(r, 1 - r, other, other, a[r, other])
            yield
            for r in range(PUB):
                ref, value = self.total(r, 1 - r, 2, 2, b[r, 2])
                ref[...] = value
                a[r] = self.send_far(r, r, 0, 4)
            yield
            for other in (1, 3):
                for r in range(PUB):
                    ref, value = self.total(r, 1 - r, other, other, b[r, other])
                    ref[...] = value
            for r in range(PUB):
                b[r] = self.send_near(r, r, 0, 4, a[r])
            yield
            for r in range(PUB):
                ref, value = self.total(r, 1 - r, 0, 0, b[r, 0])
                ref[...] = value
            for r in range(PUB):
                ref, value = self.total(r, r, 0, 4, b[r])
                self.fin[r] = value

    def give(fin, rb, ret):
        out = []
        for step in PEERS:
            p = peer(step)
            rb[p] = fin[tab[T_RANK + p]]
            out.append(push(rb.at[p], ret.at[head], seg, p))
        ret[head] = fin[tab[T_RANK + head]]
        return out

    scatter_k = Scatter(far_k, accs_k, tt_k, half_k, full_k, fin_k).steps()
    scatter_v = Scatter(far_v, accs_v, tt_v, half_v, full_v, fin_v).steps()
    run(scatter_k)
    run(scatter_v)
    run(scatter_k)
    run(scatter_k)
    run(scatter_v)
    run(scatter_k)
    run(scatter_v)
    run(scatter_k)
    give_k = give(fin_k, rb_k, ret_k)
    run(scatter_v)
    run(scatter_v)
    give_v = give(fin_v, rb_v, ret_v)
    inner = tab[T_OWN + 3] > 0

    for copies, own, ret, out in ((give_k, own_k, ret_k, dk_ref), (give_v, own_v, ret_v, dv_ref)):
        for copy in copies:
            copy.wait_recv()
        for p in range(NHEAD):
            out[0, :, p * DH:(p + 1) * DH] = (
                own[p] + jnp.where(inner, ret[p].astype(F32), 0.0)).astype(BF)

    for copy in sent:
        copy.wait_send()
    for write in writes:
        write.wait()


def body(queries, key_states, values, grad_out, owners, parents, depths, lengths):
    tab = tables_of(owners, parents, depths, lengths)
    _, slot, width = queries.shape
    kv_width = key_states.shape[2]
    any_space = pl.BlockSpec(memory_space=pl.ANY)
    vmem = pl.BlockSpec(memory_space=pltpu.VMEM)

    def blocks(n, rows=slot, dtype=BF):
        return [pltpu.VMEM((n, rows, DH), dtype)] * 2

    scratch = (
        [pltpu.VMEM((slot, width), BF)] * 2
        + [pltpu.VMEM((slot, kv_width), BF)] * 2
        + blocks(NHEAD)
        + blocks(NCOL * PUB)
        + blocks(2 * NHEAD)
        + blocks(2 * NHEAD)
        + blocks(NHEAD, dtype=F32)
        + blocks(2 * NHEAD)
        + blocks(2 * NHEAD)
        + blocks(2 * NHEAD + 1)
        + blocks(NCOL * PUB)
        + blocks(PUB * 5 * 2, slot // 2)
        + blocks(PUB * 5 * 2)
        + blocks(PUB)
        + blocks(NHEAD)
        + blocks(NHEAD)
        + [
            pltpu.VMEM((slot, width), BF),
            pltpu.VMEM((3 * slot, slot), F32),
            pltpu.VMEM((slot, DH), BF),
            pltpu.VMEM((3 * slot, DH), BF),
            pltpu.VMEM((3 * slot, DH), BF),
            pltpu.VMEM((DH, 3 * slot), BF),
            pltpu.SemaphoreType.DMA((216,)),
            pltpu.SemaphoreType.DMA((216,)),
            pltpu.SemaphoreType.DMA((4,)),
            pltpu.SemaphoreType.DMA((NHEAD,)),
        ]
    )
    return pl.pallas_call(
        kernel,
        out_shape=(
            jax.ShapeDtypeStruct(queries.shape, BF),
            jax.ShapeDtypeStruct(key_states.shape, BF),
            jax.ShapeDtypeStruct(values.shape, BF),
        ),
        in_specs=[pl.BlockSpec(memory_space=pltpu.SMEM)] + [any_space] * 4,
        out_specs=(any_space, vmem, vmem),
        scratch_shapes=scratch,
        compiler_params=pltpu.CompilerParams(
            collective_id=0, has_side_effects=True, vmem_limit_bytes=60 * 2**20),
        cost_estimate=pl.CostEstimate(
            flops=10 * QH_FLOPS * slot, bytes_accessed=10 * 2**20, transcendentals=slot * 3 * slot * width // DH),
    )(tab, queries, key_states, values, grad_out)


QH_FLOPS = 40 * 768 * 128


def solution(mesh):
    placed = (P(("seg", "head"), None, None),) * 4 + (P(),) * 4
    return jax.shard_map(
        body,
        mesh=mesh,
        in_specs=placed,
        out_specs=(P(("seg", "head"), None, None),) * 3,
        check_vma=False,
    )
```

```python
import jax
import jax.numpy as jnp
from jax import lax
from jax.experimental import pallas as pl
from jax.experimental.pallas import tpu as pltpu
from jax.sharding import PartitionSpec as P

DH = 128
PUB = 2
MESH = pl.DeviceIdType.MESH
SIDE = 4
NHEAD = 8
NCOL = 16
BF = jnp.bfloat16
F32 = jnp.float32
NEG = -1e30

T_PUB, T_ANC, T_ORDER, T_CONT, T_LAST, T_RANK, T_OWN = 0, 2, 18, 34, 50, 83, 91
T_SIZE = 96


def table_kernel(owners, parents, depths, lengths, out, inverse, shared):
    col = lax.axis_index("seg")
    mine = lax.axis_index("head")
    count = owners.shape[0]

    for g in range(count):
        inverse[owners[g]] = g
    for slot in range(count):
        if slot % NHEAD == 0:
            rank = 0
        g = inverse[slot]
        inner = g < NCOL * PUB
        place = (slot // NHEAD) * PUB + rank

        @pl.when(inner)
        def _():
            shared[g] = place

        rank = rank + inner.astype(jnp.int32)
    targets = []
    rank = 0
    for p in range(NHEAD):
        g = inverse[col * NHEAD + p]
        inner = g < NCOL * PUB
        out[T_RANK + p] = jnp.where(inner, rank, 0)

        @pl.when(inner)
        def _():
            out[T_PUB + rank] = p

        rank = rank + inner.astype(jnp.int32)
        up = parents[g]
        depth = depths[g]
        one = (depth >= 1) & (up >= 0)
        up = jnp.maximum(up, 0)
        up2 = parents[up]
        two = (depth >= 2) & one & (up2 >= 0)
        up2 = jnp.maximum(up2, 0)
        first = shared[up]
        second = shared[up2]
        out[T_ANC + 2 * p] = jnp.where(one, first, 0)
        out[T_ANC + 2 * p + 1] = jnp.where(two, second, 0)
        targets.append(jnp.where(one, first, NCOL * PUB))
        targets.append(jnp.where(two, second, NCOL * PUB))

        @pl.when(p == mine)
        def _():
            out[T_OWN] = lengths[g]
            out[T_OWN + 1] = jnp.where(one, lengths[up], 0)
            out[T_OWN + 2] = jnp.where(two, lengths[up2], 0)
            out[T_OWN + 3] = inner.astype(jnp.int32)

    n = len(targets)
    places = [0] * n
    again = [False] * n
    for b in range(n):
        for a in range(b):
            c = targets[a] <= targets[b]
            places[b] = places[b] + c.astype(jnp.int32)
            places[a] = places[a] + 1 - c.astype(jnp.int32)
            again[b] = again[b] | (targets[a] == targets[b])
    for j in range(NCOL * PUB + 1):
        out[T_LAST + j] = n
    for l in range(n):
        out[T_ORDER + places[l]] = l
        out[T_CONT + places[l]] = jnp.int32(0) + again[l]
        out[T_LAST + targets[l]] = places[l]


def tables_of(owners, parents, depths, lengths):
    smem = pl.BlockSpec(memory_space=pltpu.SMEM)
    return pl.pallas_call(
        table_kernel,
        out_shape=jax.ShapeDtypeStruct((T_SIZE,), jnp.int32),
        in_specs=[smem] * 4,
        out_specs=smem,
        scratch_shapes=[pltpu.SMEM((128,), jnp.int32), pltpu.SMEM((32,), jnp.int32)],
    )(owners, parents, depths, lengths)


PEERS = [(0, 1), (1, 0), (3, 0), (1, 1), (3, 1), (2, 0), (2, 1)]


def kernel(tab, q_ref, k_ref, v_ref, g_ref, dq_ref, dk_ref, dv_ref,
           qv, gv, kown, vown, all_k, all_v, sh_k, sh_v, sel_k, sel_v, anc_k, anc_v,
           own_k, own_v, fb_k, fb_v, far_k, far_v, accs_k, accs_v,
           half_k, half_v, full_k, full_v, fin_k, fin_v, ret_k, ret_v,
           dqv, bias, live, kc, vc, kt, ec, dcat, gs, qs, invs,
           send_sem, recv_sem, local_sem, out_sem):
    seg = lax.axis_index("seg")
    head = lax.axis_index("head")
    slot = qv.shape[0]
    mid = slot // 2
    y, x = seg // SIDE, seg % SIDE
    z, core = head // 2, head % 2

    def peer(step):
        dz, dc = step
        return ((z + dz) % SIDE) * 2 + (core + dc) % 2

    def along(axis, step):
        if axis == 0:
            return y * SIDE + (x + step) % SIDE
        return ((y + step) % SIDE) * SIDE + x

    def at(axis, da, db):
        if axis == 0:
            return ((y + db) % SIDE) * SIDE + (x + da) % SIDE
        return ((y + da) % SIDE) * SIDE + (x + db) % SIDE

    ids = [0]
    sent = []

    def push(src, dst, to_seg, to_head, owner=None):
        n = ids[0]
        ids[0] += 1
        copy = pltpu.make_async_remote_copy(
            src_ref=src, dst_ref=dst, send_sem=send_sem.at[n], recv_sem=recv_sem.at[n],
            device_id=(to_seg, to_head), device_id_type=MESH)
        copy.start()
        sent.append((owner, copy))
        return copy

    def settle(buffer):
        rest = []
        for owner, copy in sent:
            if owner is buffer:
                copy.wait_send()
            else:
                rest.append((owner, copy))
        sent[:] = rest

    barrier = pltpu.get_barrier_semaphore()
    for step in PEERS:
        pl.semaphore_signal(barrier, inc=1, device_id=(seg, peer(step)), device_id_type=MESH)
    for axis in (0, 1):
        for step in (1, 3):
            pl.semaphore_signal(barrier, inc=1, device_id=(along(axis, step), head), device_id_type=MESH)
    pl.semaphore_wait(barrier, len(PEERS) + 4)

    def lanes(p):
        return pl.ds(pl.multiple_of(p * DH, DH), DH)

    def offer(src, dst):
        return [push(src.at[0, :, lanes(peer(step))], dst.at[head], seg, peer(step)) for step in PEERS]

    first_k = offer(k_ref, all_k)
    loads = [
        pltpu.make_async_copy(src.at[0], dst, local_sem.at[n])
        for n, (src, dst) in enumerate(((k_ref, kown), (v_ref, vown), (q_ref, qv), (g_ref, gv)))
    ]
    for load in loads:
        load.start()

    length = tab[T_OWN]
    rows = lax.broadcasted_iota(jnp.int32, (slot, slot), 0)
    cols = lax.broadcasted_iota(jnp.int32, (slot, slot), 1)
    bias[0:slot, :] = jnp.where((rows <= cols) & (rows < length), 0.0, NEG)
    bias[slot:2 * slot, :] = jnp.where(rows < tab[T_OWN + 1], 0.0, NEG)
    bias[2 * slot:3 * slot, :] = jnp.where(rows < tab[T_OWN + 2], 0.0, NEG)
    row = lax.broadcasted_iota(jnp.int32, (slot, DH), 0)
    live[...] = jnp.where(row < length, 1.0, 0.0).astype(BF)

    class Gather:
        def __init__(self, sh, whole, own):
            self.sh, self.whole, self.own = sh, whole, own

        def block(self, r, da, db, part=None):
            ref = self.sh.at[at(r, da, db) * PUB + r]
            if part is None:
                return ref
            return ref.at[pl.ds(part * mid, mid)]

        def spread(self, r, axis, da, db):
            ref = self.block(r, da, db)
            return [push(ref, ref, along(axis, step), head, self.sh) for step in (1, 3)]

        def relay(self, r, axis, da, db, pair):
            out = []
            for part, copy in enumerate(pair):
                copy.wait_recv()
                step = 3 if part == 0 else 1
                ref = self.block(r, step if axis == r else da, db if axis == r else step, part)
                out.append(push(ref, ref, along(axis, 1 if part == 0 else 3), head, self.sh))
            return out

        def steps(self):
            self.whole[head] = self.own[:, lanes(head)]
            for r in range(PUB):
                self.sh[seg * PUB + r] = self.whole[tab[T_PUB + r]]
            a, b, fa, fb = {}, {}, {}, {}
            for r in range(PUB):
                a[r] = self.spread(r, r, 0, 0)
                b[r, 0] = self.spread(r, 1 - r, 0, 0)
            yield
            for r in range(PUB):
                fa[r] = self.relay(r, r, 0, 0, a[r])
                b[r, 3] = self.spread(r, 1 - r, 3, 0)
                b[r, 1] = self.spread(r, 1 - r, 1, 0)
            yield
            for r in range(PUB):
                fb[r, 0] = self.relay(r, 1 - r, 0, 0, b[r, 0])
            yield
            for r in range(PUB):
                for copy in fa[r]:
                    copy.wait_recv()
                b[r, 2] = self.spread(r, 1 - r, 2, 0)
            for r in range(PUB):
                for da in (3, 1):
                    fb[r, da] = self.relay(r, 1 - r, da, 0, b[r, da])
            yield
            for r in range(PUB):
                fb[r, 2] = self.relay(r, 1 - r, 2, 0, b[r, 2])
            yield
            for pair in fb.values():
                for copy in pair:
                    copy.wait_recv()

    def run(seq):
        for _ in seq:
            return True
        return False

    def select(sh, sel, anc):
        out = {}
        for step in PEERS:
            p = peer(step)
            for a in range(2):
                sel[p * 2 + a] = sh[tab[T_ANC + 2 * p + a]]
            out[step] = push(sel.at[pl.ds(p * 2, 2)], anc.at[pl.ds(head * 2, 2)], seg, p, sel)
        for a in range(2):
            anc[head * 2 + a] = sh[tab[T_ANC + 2 * head + a]]
        return out

    group = qv.shape[1] // kown.shape[1]
    scale = DH ** -0.5
    exp_scale = scale * 1.4426950408889634
    nt = (((1,), (1,)), ((), ()))
    order = [(0, 0)] + PEERS
    writes = []

    def arrived(got, n):
        if n > 0:
            got[((SIDE - order[n][0]) % SIDE, order[n][1])].wait_recv()

    def fill(dst, own, anc, p):
        dst[0:slot] = own[:, lanes(p)]
        for a in range(2):
            dst[(a + 1) * slot:(a + 2) * slot] = anc[p * 2 + a]

    def column(row):
        return jnp.broadcast_to(row, (DH, slot)).T

    def hand_back(terms, own, fb, far, n, p):
        own[p] = terms[0:slot]
        dst = far if n == 0 else fb
        for a in range(2):
            dst[p * 2 + a] = terms[(a + 1) * slot:(a + 2) * slot].astype(BF)
        if n == 0:
            return []
        return [push(fb.at[pl.ds(p * 2, 2)], far.at[pl.ds(head * 2, 2)], seg, p)]

    def pass_one(n):
        p = peer(order[n])
        b = n % 2
        arrived(got_k, n)
        fill(kc.at[b], kown, anc_k, p)
        for j in range(group):
            place = lanes(p * group + j)
            span = slice(j * slot, (j + 1) * slot)
            s = lax.dot_general(kc[b], qv[:, place], nt, preferred_element_type=F32) + bias[...]
            top = jnp.max(s, axis=0, keepdims=True)
            e = jnp.exp2((s - top) * exp_scale)
            inv = 1.0 / jnp.sum(e, axis=0, keepdims=True)
            ec[n, :, span] = e.astype(BF)
            invs[n, :, span] = inv
            g = (gv[:, place] * live[...]).astype(F32)
            gs[b, span] = (g * column(inv)).astype(BF)
        terms = jnp.dot(ec[n], gs[b], preferred_element_type=F32)
        return hand_back(terms, own_v, fb_v, far_v, n, p)

    def pass_two(n):
        p = peer(order[n])
        b = n % 2
        arrived(got_v, n)
        fill(kc.at[b], kown, anc_k, p)
        fill(vc.at[b], vown, anc_v, p)
        kt[b] = kc[b].T
        for j in range(group):
            place = lanes(p * group + j)
            span = slice(j * slot, (j + 1) * slot)
            g = gv[:, place] * live[...]
            wg = lax.dot_general(vc[b], g, nt, preferred_element_type=F32)
            e = ec[n, :, span].astype(F32)
            inv = invs[n, :, span]
            delta = jnp.sum(e * wg, axis=0, keepdims=True) * inv
            dcat[b, :, span] = (e * (wg - delta)).astype(BF)
            qs[b, span] = (qv[:, place].astype(F32) * column(inv)).astype(BF)
        terms = jnp.dot(dcat[b], qs[b], preferred_element_type=F32) * scale
        out = hand_back(terms, own_k, fb_k, far_k, n, p)
        dqt = jnp.dot(kt[b], dcat[b], preferred_element_type=F32) * (invs[n] * scale)
        for j in range(group):
            dqv[:, lanes(p * group + j)] = dqt[:, j * slot:(j + 1) * slot].T.astype(BF)
        wide = pl.ds(pl.multiple_of(p * (group * DH), DH), group * DH)
        write = pltpu.make_async_copy(dqv.at[:, wide], dq_ref.at[0, :, wide], out_sem.at[n])
        write.start()
        writes.append(write)
        return out

    links = 2 * NHEAD

    def sums(far, accs, tt):
        def add(n, acc):
            acc = far[tab[T_ORDER + n]].astype(F32) + acc * tab[T_CONT + n].astype(F32)
            accs[n] = acc.astype(BF)
            return acc

        lax.fori_loop(0, links, add, jnp.zeros((slot, DH), F32))
        accs[links] = jnp.zeros((slot, DH), BF)

        def spread(j, carry):
            tt[j] = accs[tab[T_LAST + j]]
            return carry

        lax.fori_loop(0, NCOL * PUB, spread, 0)

    def plus(*terms):
        total = terms[0].astype(F32)
        for term in terms[1:]:
            total = total + term.astype(F32)
        return total.astype(BF)

    class Scatter:
        def __init__(self, far, back, accs, tt, half, full, fin):
            self.far, self.back, self.accs, self.tt = far, back, accs, tt
            self.half, self.full, self.fin = half, full, fin

        def block(self, r, axis, da, db):
            return self.tt.at[at(axis, da, db) * PUB + r]

        def send_far(self, r, axis, other, slot_no):
            ref = self.block(r, axis, 2, other)
            out = []
            for part, step in ((0, 1), (1, 3)):
                out.append(push(ref.at[pl.ds(part * mid, mid)], self.half.at[(r * 5 + slot_no) * 2 + part],
                                along(axis, step), head))
            return out

        def send_near(self, r, axis, other, slot_no, pair):
            out = []
            for part, step in ((0, 1), (1, 3)):
                pair[part].wait_recv()
                ref = self.block(r, axis, step, other)
                span = pl.ds(part * mid, mid)
                ref[span] = plus(ref[span], self.half[(r * 5 + slot_no) * 2 + part])
                out.append(push(ref, self.full.at[(r * 5 + slot_no) * 2 + part], along(axis, step), head))
            return out

        def total(self, r, axis, other, slot_no, pair):
            for copy in pair:
                copy.wait_recv()
            ref = self.block(r, axis, 0, other)
            n = (r * 5 + slot_no) * 2
            return ref, plus(ref[...], self.full[n], self.full[n + 1])

        def steps(self):
            for copy in self.back:
                copy.wait_recv()
            settle(self.tt)
            sums(self.far, self.accs, self.tt)
            a, b = {}, {}
            for r in range(PUB):
                for other in (2, 1, 3, 0):
                    a[r, other] = self.send_far(r, 1 - r, other, other)
            yield
            for other in (2, 1, 3, 0):
                for r in range(PUB):
                    b[r, other] = self.send_near(r, 1 - r, other, other, a[r, other])
            yield
            for r in range(PUB):
                ref, value = self.total(r, 1 - r, 2, 2, b[r, 2])
                ref[...] = value
                a[r] = self.send_far(r, r, 0, 4)
            yield
            for other in (1, 3):
                for r in range(PUB):
                    ref, value = self.total(r, 1 - r, other, other, b[r, other])
                    ref[...] = value
            for r in range(PUB):
                b[r] = self.send_near(r, r, 0, 4, a[r])
            yield
            for r in range(PUB):
                ref, value = self.total(r, 1 - r, 0, 0, b[r, 0])
                ref[...] = value
            for r in range(PUB):
                ref, value = self.total(r, r, 0, 4, b[r])
                self.fin[r] = value

    def give(fin, rb, ret):
        out = []
        settle(rb)
        for step in PEERS:
            p = peer(step)
            rb[p] = fin[tab[T_RANK + p]]
            out.append(push(rb.at[p], ret.at[head], seg, p))
        ret[head] = fin[tab[T_RANK + head]]
        return out

    loads[0].wait()
    for copy in first_k:
        copy.wait_recv()
    first_v = offer(v_ref, all_v)
    gather_k = Gather(sh_k, all_k, kown).steps()
    gather_v = Gather(sh_v, all_v, vown).steps()
    for _ in range(4):
        run(gather_k)
    loads[1].wait()
    for copy in first_v:
        copy.wait_recv()
    run(gather_v)
    run(gather_k)
    run(gather_v)
    run(gather_k)
    got_k = select(sh_k, sel_k, anc_k)
    loads[2].wait()
    loads[3].wait()
    back_k, back_v = [], []
    for n in range(NHEAD):
        back_v += pass_one(n)
        if n < 4:
            run(gather_v)
        if n == 3:
            got_v = select(sh_v, sel_v, anc_v)
    scatter_k = Scatter(far_k, back_k, accs_k, sh_k, half_k, full_k, fin_k).steps()
    scatter_v = Scatter(far_v, back_v, accs_v, sh_v, half_v, full_v, fin_v).steps()
    for n in range(NHEAD):
        back_k += pass_two(n)
        if n >= 4:
            run(scatter_v)
    run(scatter_k)
    run(scatter_v)
    give_v = give(fin_v, sel_v, ret_v)
    for _ in range(4):
        run(scatter_k)
    give_k = give(fin_k, sel_k, ret_k)
    inner = tab[T_OWN + 3] > 0

    for copies, own, ret, out in ((give_v, own_v, ret_v, dv_ref), (give_k, own_k, ret_k, dk_ref)):
        for copy in copies:
            copy.wait_recv()
        for p in range(NHEAD):
            out[0, :, p * DH:(p + 1) * DH] = (
                own[p] + jnp.where(inner, ret[p].astype(F32), 0.0)).astype(BF)

    for _, copy in sent:
        copy.wait_send()
    for write in writes:
        write.wait()


def body(queries, key_states, values, grad_out, owners, parents, depths, lengths):
    tab = tables_of(owners, parents, depths, lengths)
    _, slot, width = queries.shape
    kv_width = key_states.shape[2]
    group = width // kv_width
    any_space = pl.BlockSpec(memory_space=pl.ANY)
    vmem = pl.BlockSpec(memory_space=pltpu.VMEM)

    def blocks(n, rows=slot, dtype=BF):
        return [pltpu.VMEM((n, rows, DH), dtype)] * 2

    scratch = (
        [pltpu.VMEM((slot, width), BF)] * 2
        + [pltpu.VMEM((slot, kv_width), BF)] * 2
        + blocks(NHEAD)
        + blocks(NCOL * PUB)
        + blocks(2 * NHEAD)
        + blocks(2 * NHEAD)
        + blocks(NHEAD, dtype=F32)
        + blocks(2 * NHEAD)
        + blocks(2 * NHEAD)
        + blocks(2 * NHEAD + 1)
        + blocks(PUB * 5 * 2, slot // 2)
        + blocks(PUB * 5 * 2)
        + blocks(PUB)
        + blocks(NHEAD)
        + [
            pltpu.VMEM((slot, width), BF),
            pltpu.VMEM((3 * slot, slot), F32),
            pltpu.VMEM((slot, DH), BF),
            pltpu.VMEM((2, 3 * slot, DH), BF),
            pltpu.VMEM((2, 3 * slot, DH), BF),
            pltpu.VMEM((2, DH, 3 * slot), BF),
            pltpu.VMEM((NHEAD, 3 * slot, group * slot), BF),
            pltpu.VMEM((2, 3 * slot, group * slot), BF),
            pltpu.VMEM((2, group * slot, DH), BF),
            pltpu.VMEM((2, group * slot, DH), BF),
            pltpu.VMEM((NHEAD, 1, group * slot), F32),
            pltpu.SemaphoreType.DMA((216,)),
            pltpu.SemaphoreType.DMA((216,)),
            pltpu.SemaphoreType.DMA((4,)),
            pltpu.SemaphoreType.DMA((NHEAD,)),
        ]
    )
    return pl.pallas_call(
        kernel,
        out_shape=(
            jax.ShapeDtypeStruct(queries.shape, BF),
            jax.ShapeDtypeStruct(key_states.shape, BF),
            jax.ShapeDtypeStruct(values.shape, BF),
        ),
        in_specs=[pl.BlockSpec(memory_space=pltpu.SMEM)] + [any_space] * 4,
        out_specs=(any_space, vmem, vmem),
        scratch_shapes=scratch,
        compiler_params=pltpu.CompilerParams(
            collective_id=0, has_side_effects=True, vmem_limit_bytes=63 * 2**20),
        cost_estimate=pl.CostEstimate(
            flops=10 * QH_FLOPS * slot, bytes_accessed=10 * 2**20, transcendentals=slot * 3 * slot * width // DH),
    )(tab, queries, key_states, values, grad_out)


QH_FLOPS = 40 * 768 * 128


def solution(mesh):
    placed = (P(("seg", "head"), None, None),) * 4 + (P(),) * 4
    return jax.shard_map(
        body,
        mesh=mesh,
        in_specs=placed,
        out_specs=(P(("seg", "head"), None, None),) * 3,
        check_vma=False,
    )
```

```python
import jax
import jax.numpy as jnp
from jax import lax
from jax.experimental import pallas as pl
from jax.experimental.pallas import tpu as pltpu
from jax.sharding import PartitionSpec as P

DH = 128
PUB = 2
MESH = pl.DeviceIdType.MESH
SIDE = 4
NHEAD = 8
NCOL = 16
BF = jnp.bfloat16
F32 = jnp.float32
NEG = -1e30

T_PUB, T_ANC, T_ORDER, T_CONT, T_LAST, T_RANK, T_OWN = 0, 2, 18, 34, 50, 83, 91
T_SIZE = 96


def table_kernel(owners, parents, depths, lengths, out, inverse, shared):
    col = lax.axis_index("seg")
    mine = lax.axis_index("head")
    count = owners.shape[0]

    for g in range(count):
        inverse[owners[g]] = g
    for slot in range(count):
        if slot % NHEAD == 0:
            rank = 0
        g = inverse[slot]
        inner = g < NCOL * PUB
        place = (slot // NHEAD) * PUB + rank

        @pl.when(inner)
        def _():
            shared[g] = place

        rank = rank + inner.astype(jnp.int32)
    targets = []
    rank = 0
    for p in range(NHEAD):
        g = inverse[col * NHEAD + p]
        inner = g < NCOL * PUB
        out[T_RANK + p] = jnp.where(inner, rank, 0)

        @pl.when(inner)
        def _():
            out[T_PUB + rank] = p

        rank = rank + inner.astype(jnp.int32)
        up = parents[g]
        depth = depths[g]
        one = (depth >= 1) & (up >= 0)
        up = jnp.maximum(up, 0)
        up2 = parents[up]
        two = (depth >= 2) & one & (up2 >= 0)
        up2 = jnp.maximum(up2, 0)
        first = shared[up]
        second = shared[up2]
        out[T_ANC + 2 * p] = jnp.where(one, first, 0)
        out[T_ANC + 2 * p + 1] = jnp.where(two, second, 0)
        targets.append(jnp.where(one, first, NCOL * PUB))
        targets.append(jnp.where(two, second, NCOL * PUB))

        @pl.when(p == mine)
        def _():
            out[T_OWN] = lengths[g]
            out[T_OWN + 1] = jnp.where(one, lengths[up], 0)
            out[T_OWN + 2] = jnp.where(two, lengths[up2], 0)
            out[T_OWN + 3] = inner.astype(jnp.int32)

    n = len(targets)
    places = [0] * n
    again = [False] * n
    for b in range(n):
        for a in range(b):
            c = targets[a] <= targets[b]
            places[b] = places[b] + c.astype(jnp.int32)
            places[a] = places[a] + 1 - c.astype(jnp.int32)
            again[b] = again[b] | (targets[a] == targets[b])
    for j in range(NCOL * PUB + 1):
        out[T_LAST + j] = n
    for l in range(n):
        out[T_ORDER + places[l]] = l
        out[T_CONT + places[l]] = jnp.int32(0) + again[l]
        out[T_LAST + targets[l]] = places[l]


def tables_of(owners, parents, depths, lengths):
    smem = pl.BlockSpec(memory_space=pltpu.SMEM)
    return pl.pallas_call(
        table_kernel,
        out_shape=jax.ShapeDtypeStruct((T_SIZE,), jnp.int32),
        in_specs=[smem] * 4,
        out_specs=smem,
        scratch_shapes=[pltpu.SMEM((128,), jnp.int32), pltpu.SMEM((32,), jnp.int32)],
    )(owners, parents, depths, lengths)


PEERS = [(0, 1), (1, 0), (1, 1), (3, 0), (3, 1), (2, 0), (2, 1)]


def kernel(tab, q_ref, k_ref, v_ref, g_ref, dq_ref, dk_ref, dv_ref,
           qv, gv, kown, vown, all_k, all_v, sh_k, sh_v, sel_k, sel_v, anc_k, anc_v,
           own_k, own_v, fb_k, fb_v, far_k, far_v, accs_k, accs_v,
           half_k, half_v, full_k, full_v, fin_k, fin_v, ret_k, ret_v,
           dqv, bias, live, kc, vc, kt, ec, dcat, gs, qs, invs,
           send_sem, recv_sem, local_sem, out_sem):
    seg = lax.axis_index("seg")
    head = lax.axis_index("head")
    slot = qv.shape[0]
    mid = slot // 2
    y, x = seg // SIDE, seg % SIDE
    z, core = head // 2, head % 2

    def peer(step):
        dz, dc = step
        return ((z + dz) % SIDE) * 2 + (core + dc) % 2

    def along(axis, step):
        if axis == 0:
            return y * SIDE + (x + step) % SIDE
        return ((y + step) % SIDE) * SIDE + x

    def at(axis, da, db):
        if axis == 0:
            return ((y + db) % SIDE) * SIDE + (x + da) % SIDE
        return ((y + da) % SIDE) * SIDE + (x + db) % SIDE

    ids = [0]
    sent = []

    class Handle:
        def __init__(self, n, like, owner=None):
            self.n, self.like, self.owner = n, like, owner

        def copy(self):
            return pltpu.make_async_remote_copy(
                src_ref=self.like, dst_ref=self.like, send_sem=send_sem.at[self.n], recv_sem=recv_sem.at[self.n],
                device_id=(seg, head), device_id_type=MESH)

        def wait_recv(self):
            self.copy().wait_recv()

        def wait_send(self):
            self.copy().wait_send()

    one_block, half_block, two_blocks = sel_k.at[0], sel_k.at[0, pl.ds(0, mid)], sel_k.at[pl.ds(0, 2)]

    def reserve(count, like):
        handles = [Handle(ids[0] + n, like) for n in range(count)]
        ids[0] += count
        sent.extend(handles)
        return handles

    def start(n, src, dst, to_seg, to_head):
        pltpu.make_async_remote_copy(
            src_ref=src, dst_ref=dst, send_sem=send_sem.at[n], recv_sem=recv_sem.at[n],
            device_id=(to_seg, to_head), device_id_type=MESH).start()

    def push(src, dst, to_seg, to_head, like, owner=None):
        handle = Handle(ids[0], like, owner)
        ids[0] += 1
        sent.append(handle)
        start(handle.n, src, dst, to_seg, to_head)
        return handle

    def settle(buffer):
        for handle in [handle for handle in sent if handle.owner is buffer]:
            handle.wait_send()
            sent.remove(handle)

    barrier = pltpu.get_barrier_semaphore()
    for step in PEERS:
        pl.semaphore_signal(barrier, inc=1, device_id=(seg, peer(step)), device_id_type=MESH)
    for axis in (0, 1):
        for step in (1, 2, 3):
            pl.semaphore_signal(barrier, inc=1, device_id=(along(axis, step), head), device_id_type=MESH)
    pl.semaphore_wait(barrier, len(PEERS) + 6)

    def lanes(p):
        return pl.ds(pl.multiple_of(p * DH, DH), DH)

    def offer(src, dst):
        return [push(src.at[0, :, lanes(peer(step))], dst.at[head], seg, peer(step), one_block) for step in PEERS]

    first_k = offer(k_ref, all_k)
    loads = [
        pltpu.make_async_copy(src.at[0], dst, local_sem.at[n])
        for n, (src, dst) in enumerate(((k_ref, kown), (v_ref, vown), (q_ref, qv), (g_ref, gv)))
    ]
    for load in loads:
        load.start()

    length = tab[T_OWN]
    rows = lax.broadcasted_iota(jnp.int32, (slot, slot), 0)
    cols = lax.broadcasted_iota(jnp.int32, (slot, slot), 1)
    bias[0:slot, :] = jnp.where((rows <= cols) & (rows < length), 0.0, NEG)
    bias[slot:2 * slot, :] = jnp.where(rows < tab[T_OWN + 1], 0.0, NEG)
    bias[2 * slot:3 * slot, :] = jnp.where(rows < tab[T_OWN + 2], 0.0, NEG)
    row = lax.broadcasted_iota(jnp.int32, (slot, DH), 0)
    live[...] = jnp.where(row < length, 1.0, 0.0).astype(BF)

    class Gather:
        def __init__(self, sh, whole, own):
            self.sh, self.whole, self.own = sh, whole, own

        def block(self, r, da, db, part=None):
            ref = self.sh.at[at(r, da, db) * PUB + r]
            if part is None:
                return ref
            return ref.at[pl.ds(part * mid, mid)]

        def spread(self, r, axis, da, db):
            ref = self.block(r, da, db)
            return [push(ref, ref, along(axis, step), head, one_block, self.sh) for step in (1, 3)]

        def relay(self, r, axis, da, db, pair):
            out = []
            for part, copy in enumerate(pair):
                copy.wait_recv()
                step = 3 if part == 0 else 1
                ref = self.block(r, step if axis == r else da, db if axis == r else step, part)
                out.append(push(ref, ref, along(axis, 1 if part == 0 else 3), head,
                                half_block, self.sh))
            return out

        def steps(self):
            self.whole[head] = self.own[:, lanes(head)]
            for r in range(PUB):
                self.sh[seg * PUB + r] = self.whole[tab[T_PUB + r]]
            a, b, relays = {}, {}, []
            for r in range(PUB):
                ref = self.block(r, 0, 0)
                a[r] = [push(ref, ref, along(r, step), head, one_block, self.sh) for step in (1, 3, 2)]
            yield
            for r in range(PUB):
                b[r, 0] = self.spread(r, 1 - r, 0, 0)
            for r in range(PUB):
                for came, da in ((0, 3), (1, 1)):
                    a[r][came].wait_recv()
                    b[r, da] = self.spread(r, 1 - r, da, 0)
            yield
            for r in range(PUB):
                relays += self.relay(r, 1 - r, 0, 0, b[r, 0])
            for r in range(PUB):
                a[r][2].wait_recv()
                b[r, 2] = self.spread(r, 1 - r, 2, 0)
            yield
            for da in (3, 1):
                for r in range(PUB):
                    relays += self.relay(r, 1 - r, da, 0, b[r, da])
            yield
            for r in range(PUB):
                relays += self.relay(r, 1 - r, 2, 0, b[r, 2])
            yield
            for copy in relays:
                copy.wait_recv()

    def run(seq):
        for _ in seq:
            return True
        return False

    def select(sh, sel, anc):
        out = []
        for step in PEERS:
            p = peer(step)
            for a in range(2):
                sel[p * 2 + a] = sh[tab[T_ANC + 2 * p + a]]
            out.append(push(sel.at[pl.ds(p * 2, 2)], anc.at[pl.ds(head * 2, 2)], seg, p, two_blocks, sel))
        for a in range(2):
            anc[head * 2 + a] = sh[tab[T_ANC + 2 * head + a]]
        return out

    group = qv.shape[1] // kown.shape[1]
    scale = DH ** -0.5
    exp_scale = scale * 1.4426950408889634
    nt = (((1,), (1,)), ((), ()))

    def giver(n):
        m = n // 2
        dz = m + m // 2 - 2 * (m // 3)
        return ((z + SIDE - dz) % SIDE) * 2 + (core + n % 2) % 2

    def fill(dst, own, anc, p):
        dst[0:slot] = own[:, lanes(p)]
        for a in range(2):
            dst[(a + 1) * slot:(a + 2) * slot] = anc[p * 2 + a]

    def column(row):
        return jnp.broadcast_to(row, (DH, slot)).T

    def hand_back(terms, own, fb, far, n, p, handles):
        own[p] = terms[0:slot]
        for a in range(2):
            fb[p * 2 + a] = terms[(a + 1) * slot:(a + 2) * slot].astype(BF)

        @pl.when(n > 0)
        def _():
            start(handles[0].n + n - 1, fb.at[pl.ds(p * 2, 2)], far.at[pl.ds(head * 2, 2)], seg, p)

    def arrived(handles, n):
        @pl.when(n > 0)
        def _():
            Handle(handles[0].n + n - 1, two_blocks).wait_recv()

    def pass_one(n, handles):
        p = giver(n)
        fill(kc, kown, anc_k, p)
        for j in range(group):
            place = lanes(p * group + j)
            span = slice(j * slot, (j + 1) * slot)
            s = lax.dot_general(kc[...], qv[:, place], nt, preferred_element_type=F32) + bias[...]
            top = jnp.max(s, axis=0, keepdims=True)
            e = jnp.exp2((s - top) * exp_scale)
            inv = 1.0 / jnp.sum(e, axis=0, keepdims=True)
            ec[n, :, span] = e.astype(BF)
            invs[n, :, span] = inv
            g = (gv[:, place] * live[...]).astype(F32)
            gs[span] = (g * column(inv)).astype(BF)
        terms = jnp.dot(ec[n], gs[...], preferred_element_type=F32)
        hand_back(terms, own_v, fb_v, far_v, n, p, handles)

    def pass_two(n, handles):
        p = giver(n)
        fill(kc, kown, anc_k, p)
        fill(vc, vown, anc_v, p)
        kt[...] = kc[...].T
        for j in range(group):
            place = lanes(p * group + j)
            span = slice(j * slot, (j + 1) * slot)
            g = gv[:, place] * live[...]
            wg = lax.dot_general(vc[...], g, nt, preferred_element_type=F32)
            e = ec[n, :, span].astype(F32)
            inv = invs[n, :, span]
            delta = jnp.sum(e * wg, axis=0, keepdims=True) * inv
            dcat[:, span] = (e * (wg - delta)).astype(BF)
            qs[span] = (qv[:, place].astype(F32) * column(inv)).astype(BF)
        terms = jnp.dot(dcat[...], qs[...], preferred_element_type=F32) * scale
        hand_back(terms, own_k, fb_k, far_k, n, p, handles)
        dqt = jnp.dot(kt[...], dcat[...], preferred_element_type=F32) * (invs[n] * scale)
        for j in range(group):
            dqv[:, lanes(p * group + j)] = dqt[:, j * slot:(j + 1) * slot].T.astype(BF)
        wide = pl.ds(pl.multiple_of(p * (group * DH), DH), group * DH)
        pltpu.make_async_copy(dqv.at[:, wide], dq_ref.at[0, :, wide], out_sem.at[n]).start()

    links = 2 * NHEAD

    def sums(far, accs, tt):
        def add(n, acc):
            acc = far[tab[T_ORDER + n]].astype(F32) + acc * tab[T_CONT + n].astype(F32)
            accs[n] = acc.astype(BF)
            return acc

        lax.fori_loop(0, links, add, jnp.zeros((slot, DH), F32))
        accs[links] = jnp.zeros((slot, DH), BF)

        def spread(j, carry):
            tt[j] = accs[tab[T_LAST + j]]
            return carry

        lax.fori_loop(0, NCOL * PUB, spread, 0)

    def plus(*terms):
        total = terms[0].astype(F32)
        for term in terms[1:]:
            total = total + term.astype(F32)
        return total.astype(BF)

    class Scatter:
        def __init__(self, far, back, fb, accs, tt, half, full, fin):
            self.fb = fb
            self.far, self.back, self.accs, self.tt = far, back, accs, tt
            self.half, self.full, self.fin = half, full, fin

        def block(self, r, axis, da, db):
            return self.tt.at[at(axis, da, db) * PUB + r]

        def send_far(self, r, axis, other, slot_no):
            ref = self.block(r, axis, 2, other)
            out = []
            for part, step in ((0, 1), (1, 3)):
                out.append(push(ref.at[pl.ds(part * mid, mid)], self.half.at[(r * 4 + slot_no) * 2 + part],
                                along(axis, step), head, half_block))
            return out

        def send_near(self, r, axis, other, slot_no, pair):
            out = []
            for part, step in ((0, 1), (1, 3)):
                pair[part].wait_recv()
                ref = self.block(r, axis, step, other)
                span = pl.ds(part * mid, mid)
                ref[span] = plus(ref[span], self.half[(r * 4 + slot_no) * 2 + part])
                out.append(push(ref, self.full.at[(r * 4 + slot_no) * 2 + part], along(axis, step), head, one_block))
            return out

        def total(self, r, axis, other, slot_no, pair):
            for copy in pair:
                copy.wait_recv()
            ref = self.block(r, axis, 0, other)
            n = (r * 4 + slot_no) * 2
            return ref, plus(ref[...], self.full[n], self.full[n + 1])

        def steps(self):
            for copy in self.back:
                copy.wait_recv()
            settle(self.tt)
            for a in range(2):
                self.far[head * 2 + a] = self.fb[head * 2 + a]
            sums(self.far, self.accs, self.tt)
            a, b = {}, {}
            for r in range(PUB):
                for other in (2, 1, 3, 0):
                    a[r, other] = self.send_far(r, 1 - r, other, other)
            yield
            for other in (2, 1, 3, 0):
                for r in range(PUB):
                    b[r, other] = self.send_near(r, 1 - r, other, other, a[r, other])
            yield
            for step in (2, 1, 3):
                for r in range(PUB):
                    ref, value = self.total(r, 1 - r, step, step, b[r, step])
                    ref[...] = value
                    a[r, 4, step] = push(ref, self.full.at[self.place(r, step)], along(r, step), head, one_block)
            yield
            for r in range(PUB):
                ref, value = self.total(r, 1 - r, 0, 0, b[r, 0])
                ref[...] = value
            yield
            for r in range(PUB):
                for step in (1, 3, 2):
                    a[r, 4, step].wait_recv()
                self.fin[r] = plus(self.block(r, r, 0, 0)[...], *[self.full[self.place(r, step)] for step in (1, 3, 2)])

        def place(self, r, step):
            return 4 * PUB * 2 + r * 3 + step - 1

    def give(fin, rb, ret):
        out = []
        settle(rb)
        for step in PEERS:
            p = peer(step)
            rb[p] = fin[tab[T_RANK + p]]
            out.append(push(rb.at[p], ret.at[head], seg, p, one_block))
        ret[head] = fin[tab[T_RANK + head]]
        return out

    loads[0].wait()
    for copy in first_k:
        copy.wait_recv()
    first_v = offer(v_ref, all_v)
    gather_k = Gather(sh_k, all_k, kown).steps()
    gather_v = Gather(sh_v, all_v, vown).steps()
    for _ in range(4):
        run(gather_k)
    loads[1].wait()
    for copy in first_v:
        copy.wait_recv()
    run(gather_v)
    run(gather_k)
    run(gather_v)
    run(gather_k)
    got_k = select(sh_k, sel_k, anc_k)
    loads[2].wait()
    loads[3].wait()
    back_v = reserve(len(PEERS), two_blocks)
    back_k = reserve(len(PEERS), two_blocks)
    got_v = []

    def first_loop(n, carry):
        arrived(got_k, n)
        pass_one(n, back_v)
        for i in range(4):
            @pl.when(n == i)
            def _():
                run(gather_v)
                if i == 3:
                    got_v.extend(select(sh_v, sel_v, anc_v))
        return carry

    lax.fori_loop(0, NHEAD, first_loop, 0)
    scatter_k = Scatter(far_k, back_k, fb_k, accs_k, sh_k, half_k, full_k, fin_k).steps()
    scatter_v = Scatter(far_v, back_v, fb_v, accs_v, sh_v, half_v, full_v, fin_v).steps()

    def second_loop(n, carry):
        arrived(got_v, n)
        pass_two(n, back_k)
        for i in range(2):
            @pl.when(n == i + 6)
            def _():
                run(scatter_v)
        return carry

    lax.fori_loop(0, NHEAD, second_loop, 0)
    run(scatter_v)
    run(scatter_k)
    run(scatter_v)
    run(scatter_k)
    run(scatter_v)
    give_v = give(fin_v, sel_v, ret_v)
    run(scatter_k)
    run(scatter_k)
    run(scatter_k)
    give_k = give(fin_k, sel_k, ret_k)
    inner = tab[T_OWN + 3] > 0

    for copies, own, ret, out in ((give_v, own_v, ret_v, dv_ref), (give_k, own_k, ret_k, dk_ref)):
        for copy in copies:
            copy.wait_recv()
        for p in range(NHEAD):
            out[0, :, p * DH:(p + 1) * DH] = (
                own[p] + jnp.where(inner, ret[p].astype(F32), 0.0)).astype(BF)

    for copy in sent:
        copy.wait_send()
    for n in range(NHEAD):
        wide = pl.ds(0, group * DH)
        pltpu.make_async_copy(dqv.at[:, wide], dq_ref.at[0, :, wide], out_sem.at[n]).wait()


def body(queries, key_states, values, grad_out, owners, parents, depths, lengths):
    tab = tables_of(owners, parents, depths, lengths)
    _, slot, width = queries.shape
    kv_width = key_states.shape[2]
    group = width // kv_width
    any_space = pl.BlockSpec(memory_space=pl.ANY)
    vmem = pl.BlockSpec(memory_space=pltpu.VMEM)

    def blocks(n, rows=slot, dtype=BF):
        return [pltpu.VMEM((n, rows, DH), dtype)] * 2

    scratch = (
        [pltpu.VMEM((slot, width), BF)] * 2
        + [pltpu.VMEM((slot, kv_width), BF)] * 2
        + blocks(NHEAD)
        + blocks(NCOL * PUB)
        + blocks(2 * NHEAD)
        + blocks(2 * NHEAD)
        + blocks(NHEAD, dtype=F32)
        + blocks(2 * NHEAD)
        + blocks(2 * NHEAD)
        + blocks(2 * NHEAD + 1)
        + blocks(PUB * 4 * 2, slot // 2)
        + blocks(PUB * (4 * 2 + 3))
        + blocks(PUB)
        + blocks(NHEAD)
        + [
            pltpu.VMEM((slot, width), BF),
            pltpu.VMEM((3 * slot, slot), F32),
            pltpu.VMEM((slot, DH), BF),
            pltpu.VMEM((3 * slot, DH), BF),
            pltpu.VMEM((3 * slot, DH), BF),
            pltpu.VMEM((DH, 3 * slot), BF),
            pltpu.VMEM((NHEAD, 3 * slot, group * slot), BF),
            pltpu.VMEM((3 * slot, group * slot), BF),
            pltpu.VMEM((group * slot, DH), BF),
            pltpu.VMEM((group * slot, DH), BF),
            pltpu.VMEM((NHEAD, 1, group * slot), F32),
            pltpu.SemaphoreType.DMA((216,)),
            pltpu.SemaphoreType.DMA((216,)),
            pltpu.SemaphoreType.DMA((4,)),
            pltpu.SemaphoreType.DMA((NHEAD,)),
        ]
    )
    return pl.pallas_call(
        kernel,
        out_shape=(
            jax.ShapeDtypeStruct(queries.shape, BF),
            jax.ShapeDtypeStruct(key_states.shape, BF),
            jax.ShapeDtypeStruct(values.shape, BF),
        ),
        in_specs=[pl.BlockSpec(memory_space=pltpu.SMEM)] + [any_space] * 4,
        out_specs=(any_space, vmem, vmem),
        scratch_shapes=scratch,
        compiler_params=pltpu.CompilerParams(
            collective_id=0, has_side_effects=True, vmem_limit_bytes=63 * 2**20),
        cost_estimate=pl.CostEstimate(
            flops=10 * QH_FLOPS * slot, bytes_accessed=10 * 2**20, transcendentals=slot * 3 * slot * width // DH),
    )(tab, queries, key_states, values, grad_out)


QH_FLOPS = 40 * 768 * 128


def solution(mesh):
    placed = (P(("seg", "head"), None, None),) * 4 + (P(),) * 4
    return jax.shard_map(
        body,
        mesh=mesh,
        in_specs=placed,
        out_specs=(P(("seg", "head"), None, None),) * 3,
        check_vma=False,
    )
```

```python
import jax
import jax.numpy as jnp
from jax import lax
from jax.experimental import pallas as pl
from jax.experimental.pallas import tpu as pltpu
from jax.sharding import PartitionSpec as P

DH = 128
PUB = 2
MESH = pl.DeviceIdType.MESH
SIDE = 4
NHEAD = 8
NCOL = 16
BF = jnp.bfloat16
F32 = jnp.float32
NEG = -1e30

T_PUB, T_ANC, T_ORDER, T_CONT, T_LAST, T_RANK, T_OWN = 0, 2, 18, 34, 50, 83, 91
T_SIZE = 96


def table_kernel(owners, parents, depths, lengths, out, inverse, shared):
    col = lax.axis_index("seg")
    mine = lax.axis_index("head")
    count = owners.shape[0]

    for g in range(count):
        inverse[owners[g]] = g
    for slot in range(count):
        if slot % NHEAD == 0:
            rank = 0
        g = inverse[slot]
        inner = g < NCOL * PUB
        place = (slot // NHEAD) * PUB + rank

        @pl.when(inner)
        def _():
            shared[g] = place

        rank = rank + inner.astype(jnp.int32)
    targets = []
    rank = 0
    for p in range(NHEAD):
        g = inverse[col * NHEAD + p]
        inner = g < NCOL * PUB
        out[T_RANK + p] = jnp.where(inner, rank, 0)

        @pl.when(inner)
        def _():
            out[T_PUB + rank] = p

        rank = rank + inner.astype(jnp.int32)
        up = parents[g]
        depth = depths[g]
        one = (depth >= 1) & (up >= 0)
        up = jnp.maximum(up, 0)
        up2 = parents[up]
        two = (depth >= 2) & one & (up2 >= 0)
        up2 = jnp.maximum(up2, 0)
        first = shared[up]
        second = shared[up2]
        out[T_ANC + 2 * p] = jnp.where(one, first, 0)
        out[T_ANC + 2 * p + 1] = jnp.where(two, second, 0)
        targets.append(jnp.where(one, first, NCOL * PUB))
        targets.append(jnp.where(two, second, NCOL * PUB))

        @pl.when(p == mine)
        def _():
            out[T_OWN] = lengths[g]
            out[T_OWN + 1] = jnp.where(one, lengths[up], 0)
            out[T_OWN + 2] = jnp.where(two, lengths[up2], 0)
            out[T_OWN + 3] = inner.astype(jnp.int32)

    n = len(targets)
    places = [0] * n
    again = [False] * n
    for b in range(n):
        for a in range(b):
            c = targets[a] <= targets[b]
            places[b] = places[b] + c.astype(jnp.int32)
            places[a] = places[a] + 1 - c.astype(jnp.int32)
            again[b] = again[b] | (targets[a] == targets[b])
    for j in range(NCOL * PUB + 1):
        out[T_LAST + j] = n
    for l in range(n):
        out[T_ORDER + places[l]] = l
        out[T_CONT + places[l]] = jnp.int32(0) + again[l]
        out[T_LAST + targets[l]] = places[l]


def tables_of(owners, parents, depths, lengths):
    smem = pl.BlockSpec(memory_space=pltpu.SMEM)
    return pl.pallas_call(
        table_kernel,
        out_shape=jax.ShapeDtypeStruct((T_SIZE,), jnp.int32),
        in_specs=[smem] * 4,
        out_specs=smem,
        scratch_shapes=[pltpu.SMEM((128,), jnp.int32), pltpu.SMEM((32,), jnp.int32)],
    )(owners, parents, depths, lengths)


PEERS = [(0, 1), (1, 0), (1, 1), (3, 0), (3, 1), (2, 0), (2, 1)]


def kernel(tab, q_ref, k_ref, v_ref, g_ref, dq_ref, dk_ref, dv_ref,
           qv, gv, kown, vown, all_k, all_v, sh_k, sh_v, sel_k, sel_v, anc_k, anc_v,
           own_k, own_v, fb_k, fb_v, far_k, far_v, accs_k, accs_v,
           half_k, half_v, full_k, full_v, fin_k, fin_v, ret_k, ret_v,
           dqv, bias, live, kc, vc, kt, ec, dcat, gs, qs, invs,
           send_sem, recv_sem, local_sem, out_sem):
    seg = lax.axis_index("seg")
    head = lax.axis_index("head")
    slot = qv.shape[0]
    mid = slot // 2
    y, x = seg // SIDE, seg % SIDE
    z, core = head // 2, head % 2

    def peer(step):
        dz, dc = step
        return ((z + dz) % SIDE) * 2 + (core + dc) % 2

    def along(axis, step):
        if axis == 0:
            return y * SIDE + (x + step) % SIDE
        return ((y + step) % SIDE) * SIDE + x

    def at(axis, da, db):
        if axis == 0:
            return ((y + db) % SIDE) * SIDE + (x + da) % SIDE
        return ((y + da) % SIDE) * SIDE + (x + db) % SIDE

    ids = [0]
    sent = []

    class Handle:
        def __init__(self, n, like, owner=None):
            self.n, self.like, self.owner = n, like, owner

        def copy(self):
            return pltpu.make_async_remote_copy(
                src_ref=self.like, dst_ref=self.like, send_sem=send_sem.at[self.n], recv_sem=recv_sem.at[self.n],
                device_id=(seg, head), device_id_type=MESH)

        def wait_recv(self):
            self.copy().wait_recv()

        def wait_send(self):
            self.copy().wait_send()

    one_block, half_block, two_blocks = sel_k.at[0], sel_k.at[0, pl.ds(0, mid)], sel_k.at[pl.ds(0, 2)]

    def reserve(count, like):
        handles = [Handle(ids[0] + n, like) for n in range(count)]
        ids[0] += count
        sent.extend(handles)
        return handles

    def start(n, src, dst, to_seg, to_head):
        pltpu.make_async_remote_copy(
            src_ref=src, dst_ref=dst, send_sem=send_sem.at[n], recv_sem=recv_sem.at[n],
            device_id=(to_seg, to_head), device_id_type=MESH).start()

    def push(src, dst, to_seg, to_head, like, owner=None):
        handle = Handle(ids[0], like, owner)
        ids[0] += 1
        sent.append(handle)
        start(handle.n, src, dst, to_seg, to_head)
        return handle

    def settle(buffer):
        for handle in [handle for handle in sent if handle.owner is buffer]:
            handle.wait_send()
            sent.remove(handle)

    barrier = pltpu.get_barrier_semaphore()
    for step in PEERS:
        pl.semaphore_signal(barrier, inc=1, device_id=(seg, peer(step)), device_id_type=MESH)
    for axis in (0, 1):
        for step in (1, 2, 3):
            pl.semaphore_signal(barrier, inc=1, device_id=(along(axis, step), head), device_id_type=MESH)
    pl.semaphore_wait(barrier, len(PEERS) + 6)

    def lanes(p):
        return pl.ds(pl.multiple_of(p * DH, DH), DH)

    def offer(src, dst):
        return [push(src.at[0, :, lanes(peer(step))], dst.at[head], seg, peer(step), one_block) for step in PEERS]

    first_k = offer(k_ref, all_k)
    loads = [
        pltpu.make_async_copy(src.at[0], dst, local_sem.at[n])
        for n, (src, dst) in enumerate(((k_ref, kown), (v_ref, vown), (q_ref, qv), (g_ref, gv)))
    ]
    for load in loads:
        load.start()

    length = tab[T_OWN]
    rows = lax.broadcasted_iota(jnp.int32, (slot, slot), 0)
    cols = lax.broadcasted_iota(jnp.int32, (slot, slot), 1)
    bias[0:slot, :] = jnp.where((rows <= cols) & (rows < length), 0.0, NEG)
    bias[slot:2 * slot, :] = jnp.where(rows < tab[T_OWN + 1], 0.0, NEG)
    bias[2 * slot:3 * slot, :] = jnp.where(rows < tab[T_OWN + 2], 0.0, NEG)
    row = lax.broadcasted_iota(jnp.int32, (slot, DH), 0)
    live[...] = jnp.where(row < length, 1.0, 0.0).astype(BF)

    class Gather:
        def __init__(self, sh, whole, own):
            self.sh, self.whole, self.own = sh, whole, own

        def block(self, r, da, db, part=None):
            ref = self.sh.at[at(r, da, db) * PUB + r]
            if part is None:
                return ref
            return ref.at[pl.ds(part * mid, mid)]

        def spread(self, r, axis, da, db):
            ref = self.block(r, da, db)
            return [push(ref, ref, along(axis, step), head, one_block, self.sh) for step in (1, 3)]

        def relay(self, r, axis, da, db, pair):
            out = []
            for part, copy in enumerate(pair):
                copy.wait_recv()
                step = 3 if part == 0 else 1
                ref = self.block(r, step if axis == r else da, db if axis == r else step, part)
                out.append(push(ref, ref, along(axis, 1 if part == 0 else 3), head,
                                half_block, self.sh))
            return out

        def steps(self):
            self.whole[head] = self.own[:, lanes(head)]
            for r in range(PUB):
                self.sh[seg * PUB + r] = self.whole[tab[T_PUB + r]]
            a, b, relays = {}, {}, []
            for r in range(PUB):
                ref = self.block(r, 0, 0)
                a[r] = [push(ref, ref, along(r, step), head, one_block, self.sh) for step in (1, 3)]
            yield
            for r in range(PUB):
                b[r, 0] = self.spread(r, 1 - r, 0, 0)
            for r in range(PUB):
                ref = self.block(r, 0, 0)
                a[r].append(push(ref, ref, along(r, 2), head, one_block, self.sh))
            for r in range(PUB):
                for came, da in ((0, 3), (1, 1)):
                    a[r][came].wait_recv()
                    b[r, da] = self.spread(r, 1 - r, da, 0)
            yield
            for r in range(PUB):
                relays += self.relay(r, 1 - r, 0, 0, b[r, 0])
            for r in range(PUB):
                a[r][2].wait_recv()
                b[r, 2] = self.spread(r, 1 - r, 2, 0)
            yield
            for da in (3, 1):
                for r in range(PUB):
                    relays += self.relay(r, 1 - r, da, 0, b[r, da])
            yield
            for r in range(PUB):
                relays += self.relay(r, 1 - r, 2, 0, b[r, 2])
            yield
            for copy in relays:
                copy.wait_recv()

    def run(seq):
        for _ in seq:
            return True
        return False

    def select(sh, sel, anc):
        out = []
        for step in PEERS:
            p = peer(step)
            for a in range(2):
                sel[p * 2 + a] = sh[tab[T_ANC + 2 * p + a]]
            out.append(push(sel.at[pl.ds(p * 2, 2)], anc.at[pl.ds(head * 2, 2)], seg, p, two_blocks, sel))
        for a in range(2):
            anc[head * 2 + a] = sh[tab[T_ANC + 2 * head + a]]
        return out

    group = qv.shape[1] // kown.shape[1]
    scale = DH ** -0.5
    exp_scale = scale * 1.4426950408889634
    nt = (((1,), (1,)), ((), ()))

    def giver(n):
        m = n // 2
        dz = m + m // 2 - 2 * (m // 3)
        return ((z + SIDE - dz) % SIDE) * 2 + (core + n % 2) % 2

    def fill(dst, own, anc, p):
        dst[0:slot] = own[:, lanes(p)]
        for a in range(2):
            dst[(a + 1) * slot:(a + 2) * slot] = anc[p * 2 + a]

    def column(row):
        return jnp.broadcast_to(row, (DH, slot)).T

    def hand_back(terms, own, fb, far, n, p, handles):
        own[p] = terms[0:slot]
        for a in range(2):
            fb[p * 2 + a] = terms[(a + 1) * slot:(a + 2) * slot].astype(BF)

        @pl.when(n > 0)
        def _():
            start(handles[0].n + n - 1, fb.at[pl.ds(p * 2, 2)], far.at[pl.ds(head * 2, 2)], seg, p)

    def arrived(handles, n):
        @pl.when(n > 0)
        def _():
            Handle(handles[0].n + n - 1, two_blocks).wait_recv()

    def pass_one(n, handles):
        p = giver(n)
        fill(kc, kown, anc_k, p)
        for j in range(group):
            place = lanes(p * group + j)
            span = slice(j * slot, (j + 1) * slot)
            s = lax.dot_general(kc[...], qv[:, place], nt, preferred_element_type=F32) + bias[...]
            top = jnp.max(s, axis=0, keepdims=True)
            e = jnp.exp2((s - top) * exp_scale)
            inv = 1.0 / jnp.sum(e, axis=0, keepdims=True)
            ec[n, :, span] = e.astype(BF)
            invs[n, :, span] = inv
            g = (gv[:, place] * live[...]).astype(F32)
            gs[span] = (g * column(inv)).astype(BF)
        terms = jnp.dot(ec[n], gs[...], preferred_element_type=F32)
        hand_back(terms, own_v, fb_v, far_v, n, p, handles)

    def pass_two(n, handles):
        p = giver(n)
        fill(kc, kown, anc_k, p)
        fill(vc, vown, anc_v, p)
        kt[...] = kc[...].T
        for j in range(group):
            place = lanes(p * group + j)
            span = slice(j * slot, (j + 1) * slot)
            g = gv[:, place] * live[...]
            wg = lax.dot_general(vc[...], g, nt, preferred_element_type=F32)
            e = ec[n, :, span].astype(F32)
            inv = invs[n, :, span]
            delta = jnp.sum(e * wg, axis=0, keepdims=True) * inv
            dcat[:, span] = (e * (wg - delta)).astype(BF)
            qs[span] = (qv[:, place].astype(F32) * column(inv)).astype(BF)
        terms = jnp.dot(dcat[...], qs[...], preferred_element_type=F32) * scale
        hand_back(terms, own_k, fb_k, far_k, n, p, handles)
        dqt = jnp.dot(kt[...], dcat[...], preferred_element_type=F32) * (invs[n] * scale)
        for j in range(group):
            dqv[:, lanes(p * group + j)] = dqt[:, j * slot:(j + 1) * slot].T.astype(BF)
        wide = pl.ds(pl.multiple_of(p * (group * DH), DH), group * DH)
        pltpu.make_async_copy(dqv.at[:, wide], dq_ref.at[0, :, wide], out_sem.at[n]).start()

    links = 2 * NHEAD

    def sums(far, accs, tt):
        def add(n, acc):
            acc = far[tab[T_ORDER + n]].astype(F32) + acc * tab[T_CONT + n].astype(F32)
            accs[n] = acc.astype(BF)
            return acc

        lax.fori_loop(0, links, add, jnp.zeros((slot, DH), F32), unroll=4)
        accs[links] = jnp.zeros((slot, DH), BF)

        def spread(j, carry):
            tt[j] = accs[tab[T_LAST + j]]
            return carry

        lax.fori_loop(0, NCOL * PUB, spread, 0, unroll=4)

    def plus(*terms):
        total = terms[0].astype(F32)
        for term in terms[1:]:
            total = total + term.astype(F32)
        return total.astype(BF)

    class Scatter:
        def __init__(self, far, back, fb, accs, tt, half, full, fin):
            self.fb = fb
            self.far, self.back, self.accs, self.tt = far, back, accs, tt
            self.half, self.full, self.fin = half, full, fin

        def block(self, r, axis, da, db):
            return self.tt.at[at(axis, da, db) * PUB + r]

        def send_far(self, r, axis, other, slot_no):
            ref = self.block(r, axis, 2, other)
            out = []
            for part, step in ((0, 1), (1, 3)):
                out.append(push(ref.at[pl.ds(part * mid, mid)], self.half.at[(r * 4 + slot_no) * 2 + part],
                                along(axis, step), head, half_block))
            return out

        def send_near(self, r, axis, other, slot_no, pair):
            out = []
            for part, step in ((0, 1), (1, 3)):
                pair[part].wait_recv()
                ref = self.block(r, axis, step, other)
                span = pl.ds(part * mid, mid)
                ref[span] = plus(ref[span], self.half[(r * 4 + slot_no) * 2 + part])
                out.append(push(ref, self.full.at[(r * 4 + slot_no) * 2 + part], along(axis, step), head, one_block))
            return out

        def total(self, r, axis, other, slot_no, pair):
            for copy in pair:
                copy.wait_recv()
            ref = self.block(r, axis, 0, other)
            n = (r * 4 + slot_no) * 2
            return ref, plus(ref[...], self.full[n], self.full[n + 1])

        def steps(self):
            for copy in self.back:
                copy.wait_recv()
            settle(self.tt)
            for a in range(2):
                self.far[head * 2 + a] = self.fb[head * 2 + a]
            sums(self.far, self.accs, self.tt)
            a, b = {}, {}
            for r in range(PUB):
                for other in (2, 1, 3, 0):
                    a[r, other] = self.send_far(r, 1 - r, other, other)
            yield
            for other in (2, 1, 3, 0):
                for r in range(PUB):
                    b[r, other] = self.send_near(r, 1 - r, other, other, a[r, other])
            yield
            for step in (2, 1, 3):
                for r in range(PUB):
                    ref, value = self.total(r, 1 - r, step, step, b[r, step])
                    ref[...] = value
                    a[r, 4, step] = push(ref, self.full.at[self.place(r, step)], along(r, step), head, one_block)
            yield
            for r in range(PUB):
                ref, value = self.total(r, 1 - r, 0, 0, b[r, 0])
                ref[...] = value
            yield
            for r in range(PUB):
                for step in (1, 3, 2):
                    a[r, 4, step].wait_recv()
                self.fin[r] = plus(self.block(r, r, 0, 0)[...], *[self.full[self.place(r, step)] for step in (1, 3, 2)])

        def place(self, r, step):
            return 4 * PUB * 2 + r * 3 + step - 1

    def give(fin, rb, ret):
        out = []
        settle(rb)
        for step in PEERS:
            p = peer(step)
            rb[p] = fin[tab[T_RANK + p]]
            out.append(push(rb.at[p], ret.at[head], seg, p, one_block))
        ret[head] = fin[tab[T_RANK + head]]
        return out

    loads[0].wait()
    for copy in first_k:
        copy.wait_recv()
    first_v = offer(v_ref, all_v)
    gather_k = Gather(sh_k, all_k, kown).steps()
    gather_v = Gather(sh_v, all_v, vown).steps()
    for _ in range(4):
        run(gather_k)
    loads[1].wait()
    for copy in first_v:
        copy.wait_recv()
    run(gather_v)
    run(gather_k)
    run(gather_v)
    run(gather_k)
    got_k = select(sh_k, sel_k, anc_k)
    loads[2].wait()
    loads[3].wait()
    back_v = reserve(len(PEERS), two_blocks)
    back_k = reserve(len(PEERS), two_blocks)
    got_v = []

    def first_loop(n, carry):
        arrived(got_k, n)
        pass_one(n, back_v)
        for i in range(4):
            @pl.when(n == i)
            def _():
                run(gather_v)
                if i == 3:
                    got_v.extend(select(sh_v, sel_v, anc_v))
        return carry

    lax.fori_loop(0, NHEAD, first_loop, 0)
    scatter_k = Scatter(far_k, back_k, fb_k, accs_k, sh_k, half_k, full_k, fin_k).steps()
    scatter_v = Scatter(far_v, back_v, fb_v, accs_v, sh_v, half_v, full_v, fin_v).steps()

    def second_loop(n, carry):
        arrived(got_v, n)
        pass_two(n, back_k)
        for i in range(2):
            @pl.when(n == i + 6)
            def _():
                run(scatter_v)
        return carry

    lax.fori_loop(0, NHEAD, second_loop, 0)
    run(scatter_v)
    run(scatter_k)
    run(scatter_v)
    run(scatter_k)
    run(scatter_v)
    give_v = give(fin_v, sel_v, ret_v)
    run(scatter_k)
    run(scatter_k)
    run(scatter_k)
    give_k = give(fin_k, sel_k, ret_k)
    inner = tab[T_OWN + 3] > 0

    for copies, own, ret, out in ((give_v, own_v, ret_v, dv_ref), (give_k, own_k, ret_k, dk_ref)):
        for copy in copies:
            copy.wait_recv()
        for p in range(NHEAD):
            out[0, :, p * DH:(p + 1) * DH] = (
                own[p] + jnp.where(inner, ret[p].astype(F32), 0.0)).astype(BF)

    for copy in sent:
        copy.wait_send()
    for n in range(NHEAD):
        wide = pl.ds(0, group * DH)
        pltpu.make_async_copy(dqv.at[:, wide], dq_ref.at[0, :, wide], out_sem.at[n]).wait()


PARTS = 4


def place_kernel(dq, dk, dv, dq_out, dk_out, dv_out):
    dq_out[...] = dq[...]
    dk_out[...] = dk[...]
    dv_out[...] = dv[...]


def body(queries, key_states, values, grad_out, owners, parents, depths, lengths):
    tab = tables_of(owners, parents, depths, lengths)
    _, slot, width = queries.shape
    kv_width = key_states.shape[2]
    group = width // kv_width
    any_space = pl.BlockSpec(memory_space=pl.ANY)
    vmem = pl.BlockSpec(memory_space=pltpu.VMEM)

    def blocks(n, rows=slot, dtype=BF):
        return [pltpu.VMEM((n, rows, DH), dtype)] * 2

    scratch = (
        [pltpu.VMEM((slot, width), BF)] * 2
        + [pltpu.VMEM((slot, kv_width), BF)] * 2
        + blocks(NHEAD)
        + blocks(NCOL * PUB)
        + blocks(2 * NHEAD)
        + blocks(2 * NHEAD)
        + blocks(NHEAD, dtype=F32)
        + blocks(2 * NHEAD)
        + blocks(2 * NHEAD)
        + blocks(2 * NHEAD + 1)
        + blocks(PUB * 4 * 2, slot // 2)
        + blocks(PUB * (4 * 2 + 3))
        + blocks(PUB)
        + blocks(NHEAD)
        + [
            pltpu.VMEM((slot, width), BF),
            pltpu.VMEM((3 * slot, slot), F32),
            pltpu.VMEM((slot, DH), BF),
            pltpu.VMEM((3 * slot, DH), BF),
            pltpu.VMEM((3 * slot, DH), BF),
            pltpu.VMEM((DH, 3 * slot), BF),
            pltpu.VMEM((NHEAD, 3 * slot, group * slot), BF),
            pltpu.VMEM((3 * slot, group * slot), BF),
            pltpu.VMEM((group * slot, DH), BF),
            pltpu.VMEM((group * slot, DH), BF),
            pltpu.VMEM((NHEAD, 1, group * slot), F32),
            pltpu.SemaphoreType.DMA((216,)),
            pltpu.SemaphoreType.DMA((216,)),
            pltpu.SemaphoreType.DMA((4,)),
            pltpu.SemaphoreType.DMA((NHEAD,)),
        ]
    )
    grads = pl.pallas_call(
        kernel,
        out_shape=(
            jax.ShapeDtypeStruct(queries.shape, BF),
            jax.ShapeDtypeStruct(key_states.shape, BF),
            jax.ShapeDtypeStruct(values.shape, BF),
        ),
        in_specs=[pl.BlockSpec(memory_space=pltpu.SMEM)] + [any_space] * 4,
        out_specs=(any_space, vmem, vmem),
        scratch_shapes=scratch,
        compiler_params=pltpu.CompilerParams(
            collective_id=0, has_side_effects=True, vmem_limit_bytes=63 * 2**20),
        cost_estimate=pl.CostEstimate(
            flops=10 * QH_FLOPS * slot, bytes_accessed=10 * 2**20, transcendentals=slot * 3 * slot * width // DH),
    )(tab, queries, key_states, values, grad_out)
    blocks_of = [pl.BlockSpec((1, slot // PARTS, grad.shape[2]), lambda i: (0, i, 0)) for grad in grads]
    return pl.pallas_call(
        place_kernel,
        grid=(PARTS,),
        out_shape=tuple(jax.ShapeDtypeStruct(grad.shape, BF) for grad in grads),
        in_specs=blocks_of,
        out_specs=tuple(blocks_of),
    )(*grads)


QH_FLOPS = 40 * 768 * 128


def solution(mesh):
    placed = (P(("seg", "head"), None, None),) * 4 + (P(),) * 4
    return jax.shard_map(
        body,
        mesh=mesh,
        in_specs=placed,
        out_specs=(P(("seg", "head"), None, None),) * 3,
        check_vma=False,
    )
```
